512 devices in a mesh: segment: 16 (over z_lo, x), shard: 32 (over y, z_hi, core).
Axes of the slice: x: 4, y: 8, z: 8 (z_hi: 2, z_lo: 4; z = z_hi * 4 + z_lo), core: 2. Of those that a mesh axis runs over, the one named last changes fastest.
Arguments:
- value_weight: bfloat16 [16, 8192, 4096], P('segment', 'shard'), as said below
- output_weight: bfloat16 [16, 4096, 8192], P('segment', None, 'shard'), as said below
- norm_gain: float32 [16, 8192], P('segment', 'shard'), may hold values from 0.1 to 1.9
- arriving: bfloat16 [16, 128, 8192], P('segment', None, 'shard'), may hold values from -6 to 6
- fresh_inputs: bfloat16 [1, 128, 8192], P(None, None, 'shard'), may hold values from -6 to 6
- returning: bfloat16 [16, 128, 8192], P('segment', None, 'shard'), may hold values from -8 to 8
- cotangents: bfloat16 [1, 128, 8192], P(None, None, 'shard'), may hold values from -8 to 8
- saved_inputs: bfloat16 [16, 2, 128, 8192], P('segment', None, None, 'shard'), may hold values from -8 to 8
- forward_base: bfloat16 [16, 8, 64, 8192], P('segment', None, None, 'shard'), may hold values from -6 to 6
- backward_base: bfloat16 [16, 8, 64, 8192], P('segment', None, None, 'shard'), may hold values from -8 to 8
- sample_ids: int32 [17, 2], replicated, may hold values from 0 to 7
- forward_exponents: int32 [16, 2, 64], P('segment', None, 'shard'), may hold values from -7 to -3
- backward_exponents: int32 [16, 2, 64], P('segment', None, 'shard'), may hold values from -7 to -3
Outputs:
- segment_outputs: bfloat16 [16, 128, 8192], P('segment', None, 'shard')
- input_grads: bfloat16 [16, 128, 8192], P('segment', None, 'shard')
- gain_grads: float32 [16, 8192], P('segment', 'shard')
The draws below stay inside these ranges and needn't reach their ends.
Inputs may be any that keep to these rules, and one draw needn't show every extreme that they name: `value_weight`: entries of order the inverse square root of 8192. `output_weight`: entries of order the inverse square root of 4096.
All inputs are finite; a program needn't handle non-finite values.
Results may differ from the reference program's by a relative error of at most 0.025.
Values may be sent and summed in bfloat16 or wider, within the bound.
No kernel may reach another device: no remote copies, remote signals or barrier semaphores. Data moves between devices by JAX's collectives and lax.ppermute only.
A program may use at most 64 MiB of HBM per device.

```python
import math
import jax
import jax.numpy as jnp
from jax import lax

D = 8192
H = 4096
BLOCK = 128
BLOCKS = 64
SEQ = 64
SPM = 2
M = 128
SLOTS = 8
TICKS = 2
MICRO = 17
N_SEGMENT = 16
N_SHARD = 32


shared_part = 0.8


def common_rows(key):
    key = jax.random.fold_in(key, 71)
    first_key, second_key = jax.random.split(key)
    rows = 0.8 * jax.random.truncated_normal(first_key, -4.0, 4.0, (SEQ, D), jnp.float32)
    spread = jax.random.uniform(second_key, (SEQ, 1), jnp.float32, 0.0, 1e-06)
    return rows * jnp.exp(spread)


def weight_core(key):
    key = jax.random.fold_in(key, 211)
    return jax.random.truncated_normal(key, -4.0, 4.0, (N_SEGMENT, H, D), jnp.float32)


def draw_value_weight(key, part):
    core = weight_core(key)
    return (jnp.swapaxes(core, 1, 2) * D ** (-0.5)).astype(jnp.bfloat16)


def draw_output_weight(key, part):
    core = weight_core(key)
    key = jax.random.fold_in(key, 6)
    own = jax.random.truncated_normal(key, -4.0, 4.0, (N_SEGMENT, H, D), jnp.float32)
    mixed = shared_part * core + math.sqrt(1.0 - shared_part * shared_part) * own
    return (mixed * H ** (-0.5)).astype(jnp.bfloat16)


def draw_returning(key, part):
    shared = jnp.tile(common_rows(key), (SPM, 1))
    key = jax.random.fold_in(key, 7)
    noise = 0.6 * jax.random.truncated_normal(key, -4.0, 4.0, (N_SEGMENT, SPM * SEQ, D), jnp.float32)
    return jnp.clip(shared[None] + noise, -8.0, 8.0).astype(jnp.bfloat16)


def draw_cotangents(key, part):
    shared = jnp.tile(common_rows(key), (SPM, 1))
    key = jax.random.fold_in(key, 8)
    noise = 0.6 * jax.random.truncated_normal(key, -4.0, 4.0, (TICKS - 1, SPM * SEQ, D), jnp.float32)
    return jnp.clip(shared[None] + noise, -8.0, 8.0).astype(jnp.bfloat16)


def draw_saved_inputs(key, part):
    shared = jnp.tile(common_rows(key), (SPM, 1))
    key = jax.random.fold_in(key, 9)
    noise = 0.5 * jax.random.truncated_normal(key, -4.0, 4.0, (N_SEGMENT, TICKS, SPM * SEQ, D), jnp.float32)
    return jnp.clip(shared[None, None] + noise, -8.0, 8.0).astype(jnp.bfloat16)


def draw_backward_base(key, part):
    shared = common_rows(key)
    key = jax.random.fold_in(key, 10)
    noise = 0.6 * jax.random.truncated_normal(key, -4.0, 4.0, (N_SEGMENT, SLOTS, SEQ, D), jnp.float32)
    return jnp.clip(shared[None, None] + noise, -8.0, 8.0).astype(jnp.bfloat16)


def place_ends(values, rng, least, high):
    longest = values.shape.index(max(values.shape))
    spots = []
    for shift in (0, 1):
        where = [jax.random.randint(jax.random.fold_in(rng, axis), (), 0, length) for axis, length in enumerate(values.shape)]
        where[longest] = (where[longest] + shift) % values.shape[longest]
        spots.append(tuple(where))
    return values.at[spots[0]].set(least).at[spots[1]].set(high)


def levels(rng, shape, cuts, smallest, top_value):
    def one(axis_at, blocks):
        steps = jax.random.uniform(jax.random.fold_in(jax.random.fold_in(rng, 6), axis_at), (blocks,), jnp.float32, smallest / len(cuts), top_value / len(cuts))
        return jnp.repeat(jnp.exp(steps), shape[axis_at] // blocks).reshape((-1,) + (1,) * (len(shape) - axis_at - 1))

    gain = one(*cuts[0])
    for cut in cuts[1:]:
        gain = gain * one(*cut)
    return gain


def scatter_about(rng, dims, width, limit, cuts=(), held_as=jnp.bfloat16):
    drawn = width * jax.random.normal(rng, dims, jnp.float32)
    if cuts:
        drawn = drawn * levels(rng, dims, cuts, -0.22, 0.18)
    return jnp.clip(drawn, -limit, limit).astype(held_as)


def setup_inputs(seed: int = 0) -> dict:
    keys = jax.random.split(jax.random.key(seed), 14)
    return {
        "value_weight": draw_value_weight(jax.random.fold_in(keys[13], 71), 0),
        "output_weight": draw_output_weight(jax.random.fold_in(keys[13], 71), 0),
        "norm_gain": jnp.clip(1.0 + 0.18 * jax.random.normal(keys[2], (N_SEGMENT, D), jnp.float32), 0.1, 1.9),
        "arriving": scatter_about(keys[3], (N_SEGMENT, SPM * SEQ, D), 1.0, 6.0, ((0, 16), (2, 32))),
        "fresh_inputs": scatter_about(keys[4], (TICKS - 1, SPM * SEQ, D), 1.0, 6.0, ((2, 32),)),
        "returning": draw_returning(jax.random.fold_in(keys[13], 71), 0),
        "cotangents": draw_cotangents(jax.random.fold_in(keys[13], 71), 0),
        "saved_inputs": draw_saved_inputs(jax.random.fold_in(keys[13], 71), 0),
        "forward_base": scatter_about(keys[8], (N_SEGMENT, SLOTS, SEQ, D), 1.0, 6.0, ((0, 16), (3, 32))),
        "backward_base": draw_backward_base(jax.random.fold_in(keys[13], 71), 0),
        "sample_ids": place_ends(jax.random.randint(keys[10], (MICRO, SPM), 0, SLOTS), jax.random.fold_in(keys[10], 1), 0, SLOTS - 1).astype(jnp.int32),
        "forward_exponents": place_ends(jax.random.randint(keys[11], (N_SEGMENT, TICKS, BLOCKS), -7, -2), jax.random.fold_in(keys[11], 1), -7, (-2) - 1).astype(jnp.int32),
        "backward_exponents": place_ends(jax.random.randint(keys[12], (N_SEGMENT, TICKS, BLOCKS), -7, -2), jax.random.fold_in(keys[12], 1), -7, (-2) - 1).astype(jnp.int32),
    }


norm_epsilon = 1e-05

def power_two(exponent):
    magnitude = jnp.abs(exponent)
    factor = jnp.ones(exponent.shape, jnp.float32)
    for bit_number in range(4):
        bit_set = magnitude // 2 ** bit_number % 2 == 1
        factor = jnp.where(bit_set, factor * 2.0 ** 2 ** bit_number, factor)
    return jnp.where(exponent < 0, 1.0 / factor, factor)

def decode_message(message, base_rows, exponents):
    leading = message.shape[:-1]
    features = message.shape[-1]
    shaped = leading + (features // BLOCK, BLOCK)
    block_scale = power_two(exponents)[..., None]
    block_inverse = power_two(-exponents)[..., None]
    base_float = base_rows.astype(jnp.float32).reshape(shaped)
    change = message.astype(jnp.float32).reshape(shaped) - base_float
    coded_delta = jnp.clip(change * block_inverse, -127.0, 127.0).astype(jnp.bfloat16)
    rebuilt = base_float + coded_delta.astype(jnp.float32) * block_scale
    return rebuilt.reshape(message.shape).astype(jnp.bfloat16)

def forward_layer(packed):
    inputs_now, gain_row, value_matrix, output_matrix = packed
    width_share = D // N_SHARD
    inputs_float = inputs_now.astype(jnp.float32)
    scaled = (inputs_float * gain_row).astype(jnp.bfloat16)
    factor = lax.rsqrt(lax.optimization_barrier(jnp.mean(inputs_float * inputs_float, axis=-1)) + norm_epsilon)[:, None]
    pieces = scaled.astype(jnp.float32).reshape(M, N_SHARD, width_share)
    weights = value_matrix.astype(jnp.float32).reshape(N_SHARD, width_share, H)
    partials = jnp.einsum('mnc,nch->nmh', pieces, weights)
    rounded = lax.optimization_barrier(partials.astype(jnp.bfloat16)).astype(jnp.float32)
    pre = (factor * lax.optimization_barrier(jnp.sum(rounded, axis=0))).astype(jnp.bfloat16)
    branch = jnp.dot(pre, output_matrix, preferred_element_type=jnp.float32)
    return (inputs_float + branch).astype(jnp.bfloat16)

def backward_layer(packed):
    grad_now, saved_now, gain_row, value_matrix, output_matrix = packed
    width_share = D // N_SHARD
    pieces = grad_now.astype(jnp.float32).reshape(M, N_SHARD, width_share)
    weights = output_matrix.astype(jnp.float32).reshape(H, N_SHARD, width_share)
    partials = jnp.einsum('mnc,hnc->nmh', pieces, weights)
    rounded = lax.optimization_barrier(partials.astype(jnp.bfloat16)).astype(jnp.float32)
    value_grad = lax.optimization_barrier(jnp.sum(rounded, axis=0)).astype(jnp.bfloat16)
    scaled_grad = jnp.dot(value_grad, value_matrix.T, preferred_element_type=jnp.float32)
    saved_float = saved_now.astype(jnp.float32)
    factor = lax.rsqrt(lax.optimization_barrier(jnp.mean(saved_float * saved_float, axis=-1)) + norm_epsilon)[:, None]
    row_dot = lax.optimization_barrier(jnp.sum(saved_float * gain_row * scaled_grad, axis=-1))[:, None]
    grad_float = grad_now.astype(jnp.float32)
    grad_out = (grad_float + factor * gain_row * scaled_grad - saved_float * factor ** 3 * row_dot / D).astype(jnp.bfloat16)
    gain_part = lax.optimization_barrier(jnp.sum(scaled_grad * saved_float * factor, axis=0))
    return (grad_out, gain_part)

def reference(value_weight, output_weight, norm_gain, arriving, fresh_inputs, returning, cotangents, saved_inputs, forward_base, backward_base, sample_ids, forward_exponents, backward_exponents):
    segment_range = jnp.arange(N_SEGMENT, dtype=jnp.int32)
    gain_total = jnp.zeros((N_SEGMENT, D), jnp.float32)
    segment_out = arriving
    grad_out = returning
    for tick_index in range(TICKS):
        if tick_index == 0:
            forward_in = arriving
            backward_in = returning
        else:
            forward_in = jnp.concatenate([fresh_inputs[tick_index - 1][None], segment_out[:-1]], axis=0)
            backward_in = jnp.concatenate([grad_out[1:], cotangents[tick_index - 1][None]], axis=0)
        forward_ids = sample_ids[(tick_index - segment_range + N_SEGMENT - 1).astype(jnp.int32)]
        forward_rows = forward_base[segment_range[:, None], forward_ids].reshape(N_SEGMENT, M, D)
        inputs_now = decode_message(forward_in, forward_rows, forward_exponents[:, tick_index][:, None, :])
        segment_out = lax.map(forward_layer, (inputs_now, norm_gain, value_weight, output_weight))
        backward_ids = sample_ids[(tick_index + segment_range).astype(jnp.int32)]
        backward_rows = backward_base[segment_range[:, None], backward_ids].reshape(N_SEGMENT, M, D)
        grad_now = decode_message(backward_in, backward_rows, backward_exponents[:, tick_index][:, None, :])
        grad_out, gain_parts = lax.map(backward_layer, (grad_now, saved_inputs[:, tick_index], norm_gain, value_weight, output_weight))
        gain_total = gain_total + gain_parts
    return (segment_out, grad_out, gain_total)
```

```python
import functools

import jax
import jax.numpy as jnp
from jax import lax
from jax.experimental import pallas as pl
from jax.experimental.pallas import tpu as pltpu
from jax.sharding import PartitionSpec as P

D = 8192
BLOCK = 128
ROWS = 128
WIDTH = 256
SEQ = 64
STATS = 16
RING = 8
HALF = RING * WIDTH
EPSILON = 1e-05
F32 = jnp.float32
BF16 = jnp.bfloat16
VMEM_LIMIT = 20 * 1024 * 1024


def core_pairs():
    return [(index, index ^ 1) for index in range(4 * RING)]


def z_pairs():
    return [(index, index ^ 2) for index in range(4 * RING)]


def rings():
    return [[4 * y + rest for y in range(RING)] for rest in range(4)]


def swapped(value, groups=None):
    return lax.all_to_all(value, "shard", 0, 0, axis_index_groups=groups, tiled=True)


def shifted(value, axis, steps):
    count = lax.axis_size(axis)
    leading, last = (max(0, -steps), min(count, count - steps))
    return lax.ppermute(value, axis, [(source, source + steps) for source in range(leading, last)])


def call(kernel, name, outs, *, prefetch=(), blocks=None, flops=0, operands=()):
    blocks = blocks or {}

    def spec(position, operand):
        if position in blocks:
            shape, index_map = blocks[position]
            return pl.BlockSpec(shape, index_map)
        rank = len(operand.shape)
        return pl.BlockSpec(operand.shape, lambda *_: (0,) * rank)

    moved = 0
    for position, operand in enumerate(operands):
        shape = blocks[position][0] if position in blocks else operand.shape
        size = 1
        for length in shape:
            size *= length
        moved += size * operand.dtype.itemsize
    for out in outs:
        moved += out.size * out.dtype.itemsize
    return pl.pallas_call(
        kernel,
        out_shape=outs,
        grid_spec=pltpu.PrefetchScalarGridSpec(
            num_scalar_prefetch=len(prefetch),
            grid=(1,),
            in_specs=[spec(position, operand) for position, operand in enumerate(operands)],
            out_specs=[pl.BlockSpec(out.shape, lambda *_, rank=len(out.shape): (0,) * rank) for out in outs],
        ),
        compiler_params=pltpu.CompilerParams(vmem_limit_bytes=VMEM_LIMIT),
        cost_estimate=pl.CostEstimate(flops=flops, bytes_accessed=moved, transcendentals=0),
        name=name,
    )(*prefetch, *operands)


def shape_of(*dims, dtype=BF16):
    return jax.ShapeDtypeStruct(dims, dtype)


def across(column):
    return jnp.broadcast_to(column, (ROWS, ROWS)).T[0:1]


def down(row):
    square = jnp.broadcast_to(row, (ROWS, ROWS)).T
    return jnp.concatenate([square, square], axis=1)


def split_stats(total):
    high = total.astype(BF16).astype(F32)
    return jnp.concatenate([high, total - high], axis=1).astype(BF16)


def joined_stats(coded):
    value = coded.astype(F32)
    return value[:, :ROWS] + value[:, ROWS:]


def power_row(low, high, sign):
    lane = lax.broadcasted_iota(jnp.int32, (1, WIDTH), 1)
    exponent = sign * jnp.where(lane < BLOCK, low, high)
    magnitude = jnp.abs(exponent)
    grown = jnp.ones((1, WIDTH), F32)
    shrunk = jnp.ones((1, WIDTH), F32)
    for bit in range(4):
        bit_set = (magnitude >> bit) & 1 == 1
        grown = jnp.where(bit_set, grown * 2.0 ** (2**bit), grown)
        shrunk = jnp.where(bit_set, shrunk * 0.5 ** (2**bit), shrunk)
    return jnp.where(exponent < 0, shrunk, grown)


def decoded(message, first_ref, second_ref, exponents, tick):
    low, high = exponents[tick, 0], exponents[tick, 1]
    scale = power_row(low, high, 1)
    inverse = power_row(low, high, -1)
    base = jnp.concatenate([first_ref[0], second_ref[0]], axis=0).astype(F32)
    delta = jnp.clip((message.astype(F32) - base) * inverse, -127.0, 127.0).astype(BF16)
    return (base + delta.astype(F32) * scale).astype(BF16)


def chosen(meta, edge, refs):
    if len(refs) == 1:
        return refs[0][...]
    return jnp.where(meta[0] == edge, refs[1][0].astype(F32), refs[0][...].astype(F32))


def forward_start(tick, messages, ids, meta, exponents, *refs):
    given, refs = refs[:messages], refs[messages:]
    first, second, gain, weight, x_out, keep, send = refs
    x = decoded(chosen(meta, 0, given), first, second, exponents, tick)
    x_out[...] = x
    x = x.astype(F32)
    scaled = (x * gain[...]).astype(BF16)
    total = across(jnp.sum(x * x, axis=1, keepdims=True))
    stats = split_stats(jnp.broadcast_to(total, (STATS, ROWS)))
    core = meta[3]
    for out, half in ((send, 1 - core), (keep, core)):
        for j in range(RING):
            at = pl.multiple_of((half * RING + j) * WIDTH, WIDTH)
            part = jnp.dot(scaled, weight[:, pl.ds(at, WIDTH)], preferred_element_type=F32)
            out[j, :ROWS] = part.astype(BF16)
            out[j, ROWS:] = stats


def backward_start(tick, messages, last, ids, meta, exponents, *refs):
    given, refs = refs[:messages], refs[messages:]
    if tick == 0:
        first, second, weight, saved, g_out, keep, send = refs
        rows = []
        for k in range(2):
            value = saved[k].astype(F32)
            rows.append(jnp.broadcast_to(across(jnp.sum(value * value, axis=1, keepdims=True)), (STATS // 2, ROWS)))
        stats = split_stats(jnp.concatenate(rows, axis=0))
    else:
        first, second, weight, g_out, keep, send = refs
        stats = None
    g = decoded(chosen(meta, last, given), first, second, exponents, tick).astype(BF16)
    g_out[...] = g
    core = meta[3]
    for out, half in ((send, 1 - core), (keep, core)):
        for j in range(RING):
            at = pl.multiple_of((half * RING + j) * WIDTH, WIDTH)
            part = lax.dot_general(
                g, weight[pl.ds(at, WIDTH), :], (((1,), (1,)), ((), ())), preferred_element_type=F32
            )
            out[j, :ROWS] = part.astype(BF16)
            if stats is not None:
                out[j, ROWS:] = stats


def core_sum(keep, other, out):
    extra = keep.shape[1] > ROWS
    if extra:
        stats = split_stats(joined_stats(keep[0, ROWS:]) + joined_stats(other[0, ROWS:]))
    for j in range(RING):
        out[j, :ROWS] = (keep[j, :ROWS].astype(F32) + other[j, :ROWS].astype(F32)).astype(BF16)
        if extra:
            out[j, ROWS:] = stats


def ring_sum(pieces, out):
    total = pieces[0, :ROWS].astype(F32)
    for j in range(1, RING):
        total = total + pieces[j, :ROWS].astype(F32)
    out[:ROWS] = total.astype(BF16)
    if out.shape[0] > ROWS:
        stats = joined_stats(pieces[0, ROWS:])
        for j in range(1, RING):
            stats = stats + joined_stats(pieces[j, ROWS:])
        out[ROWS:] = split_stats(stats)


def forward_share(own, other, out):
    total = joined_stats(own[ROWS:]) + joined_stats(other[ROWS:])
    factor = lax.rsqrt(total[0:1] / D + EPSILON)
    value = own[:ROWS].astype(F32) + other[:ROWS].astype(F32)
    out[...] = jnp.broadcast_to((down(factor) * value).astype(BF16)[None], out.shape)


def backward_share(own, other, out, *stats):
    value = (own[:ROWS].astype(F32) + other[:ROWS].astype(F32)).astype(BF16)
    out[...] = jnp.broadcast_to(value[None], out.shape)
    if stats:
        stats[0][...] = joined_stats(own[ROWS:]) + joined_stats(other[ROWS:])


def forward_product(meta, blocks, own_weight, other_weight, mine, others):
    for weight, out in ((other_weight, others), (own_weight, mine)):
        total = jnp.zeros((ROWS, WIDTH), F32)
        for j in range(RING):
            at = j * WIDTH
            total = total + jnp.dot(blocks[j], weight[pl.ds(at, WIDTH), :], preferred_element_type=F32)
        out[...] = total


def backward_product(meta, blocks, own_weight, other_weight, mine, others):
    for weight, out in ((other_weight, others), (own_weight, mine)):
        total = jnp.zeros((ROWS, WIDTH), F32)
        for j in range(RING):
            at = j * WIDTH
            total = total + lax.dot_general(
                blocks[j], weight[:, pl.ds(at, WIDTH)], (((1,), (1,)), ((), ())), preferred_element_type=F32
            )
        out[...] = total


def forward_end(x, mine, other, out):
    out[...] = (x[...].astype(F32) + (mine[...] + other[...])).astype(BF16)


def saved_scale(stats, tick):
    at = tick * (STATS // 2)
    return down(lax.rsqrt(stats[at : at + 1] / D + EPSILON))


def backward_middle(tick, mine, other, saved, gain, stats, *refs):
    before, (scaled_grad, row_dot, gain_out) = refs[:-3], refs[-3:]
    value = mine[...] + other[...]
    scaled_grad[...] = value
    kept = saved[0].astype(F32)
    dots = jnp.sum(kept * gain[...] * value, axis=1, keepdims=True)
    row_dot[...] = jnp.broadcast_to(across(dots), row_dot.shape)
    total = jnp.sum(value * kept * saved_scale(stats, tick), axis=0, keepdims=True)
    gain_out[...] = total + before[0][...] if before else total


def backward_end(tick, g, scaled_grad, saved, gain, stats, *refs):
    dots, out = refs
    total = dots[0, 0:1]
    for j in range(1, dots.shape[0]):
        total = total + dots[j, 0:1]
    factor = saved_scale(stats, tick)
    value = g[...].astype(F32) + factor * gain[...] * scaled_grad[...]
    out[...] = (value - saved[0].astype(F32) * (factor * factor * factor) * down(total) / D).astype(BF16)


def scattered(keep, send):
    rows = keep.shape[1]
    other = lax.ppermute(send, "shard", core_pairs())
    (pieces,) = call(core_sum, "core_sum", [shape_of(RING, rows, WIDTH)], operands=(keep, other))
    (own,) = call(ring_sum, "ring_sum", [shape_of(rows, WIDTH)], operands=(swapped(pieces, rings()),))
    return own, lax.ppermute(own, "shard", z_pairs())


def shards(
    value_weight,
    output_weight,
    norm_gain,
    arriving,
    fresh_inputs,
    returning,
    cotangents,
    saved_inputs,
    forward_base,
    backward_base,
    sample_ids,
    forward_exponents,
    backward_exponents,
):
    segment = lax.axis_index("segment")
    segments = lax.axis_size("segment")
    position = lax.axis_index("shard")
    core = position % 2
    meta = jnp.stack([segment, position // 4, position // 2 % 2, core]).astype(jnp.int32)
    value_local, output_local = value_weight[0], output_weight[0]
    saved, ticks = saved_inputs[0], saved_inputs.shape[1]
    half = (1 - core) * HALF
    value_other = lax.ppermute(
        lax.dynamic_slice(value_local, (0, half), (WIDTH, HALF)), "shard", core_pairs()
    )
    output_other = lax.ppermute(
        lax.dynamic_slice(output_local, (half, 0), (HALF, WIDTH)), "shard", core_pairs()
    )
    piece = shape_of(ROWS, WIDTH)
    wide = shape_of(ROWS, WIDTH, dtype=F32)
    start_flops = 2 * ROWS * WIDTH * 2 * HALF

    def base_blocks(first, micro):
        return {
            first + sample: (
                (1, SEQ, WIDTH),
                lambda i, ids, meta, exps, sample=sample: (ids[micro(meta), sample], 0, 0),
            )
            for sample in range(2)
        }

    forward_message, backward_message = [arriving[0]], [returning[0]]
    stats = gain_total = None
    for tick in range(ticks):
        tall = shape_of(RING, ROWS + STATS, WIDTH)
        count = len(forward_message)
        x, keep, send = call(
            functools.partial(forward_start, tick, count),
            "forward_start",
            [piece, tall, tall],
            prefetch=(sample_ids, meta, forward_exponents[0]),
            operands=(*forward_message, forward_base[0], forward_base[0], norm_gain, value_local),
            blocks=base_blocks(count, lambda meta: tick - meta[0] + segments - 1),
            flops=start_flops,
        )
        low = tall if tick == 0 else shape_of(RING, ROWS, WIDTH)
        operands = (*backward_message, backward_base[0], backward_base[0], output_local)
        g, back_keep, back_send = call(
            functools.partial(backward_start, tick, count, segments - 1),
            "backward_start",
            [piece, low, low],
            prefetch=(sample_ids, meta, backward_exponents[0]),
            operands=operands + ((saved,) if tick == 0 else ()),
            blocks=base_blocks(count, lambda meta: tick + meta[0]),
            flops=start_flops,
        )
        own, other = scattered(keep, send)
        back_own, back_other = scattered(back_keep, back_send)

        copies = shape_of(RING, ROWS, WIDTH)
        (pre,) = call(forward_share, "forward_share", [copies], operands=(own, other))
        gathered = swapped(pre, rings())
        share_outs = [copies] + ([shape_of(STATS, ROWS, dtype=F32)] if tick == 0 else [])
        value_grad, *given = call(
            backward_share, "backward_share", share_outs, operands=(back_own, back_other)
        )
        stats = given[0] if given else stats
        back_gathered = swapped(value_grad, rings())

        mine, others = call(
            forward_product,
            "forward_product",
            [wide, wide],
            prefetch=(meta,),
            operands=(gathered, output_local, output_other),
            blocks={1: ((HALF, WIDTH), lambda i, meta: (meta[3], 0))},
            flops=start_flops,
        )
        (segment_out,) = call(
            forward_end,
            "forward_end",
            [piece],
            operands=(x, mine, lax.ppermute(others, "shard", core_pairs())),
        )
        if tick + 1 < ticks:
            forward_message = [shifted(segment_out, "segment", 1), fresh_inputs[tick : tick + 1]]

        mine, others = call(
            backward_product,
            "backward_product",
            [wide, wide],
            prefetch=(meta,),
            operands=(back_gathered, value_local, value_other),
            blocks={1: ((WIDTH, HALF), lambda i, meta: (0, meta[3]))},
            flops=start_flops,
        )
        saved_block = {2: ((1, ROWS, WIDTH), lambda i, tick=tick: (tick, 0, 0))}
        before = () if gain_total is None else (gain_total,)
        small = shape_of(4 * RING, 8, ROWS, dtype=F32)
        scaled_grad, dots, gain_total = call(
            functools.partial(backward_middle, tick),
            "backward_middle",
            [wide, small, shape_of(1, WIDTH, dtype=F32)],
            operands=(mine, lax.ppermute(others, "shard", core_pairs()), saved, norm_gain, stats) + before,
            blocks=saved_block,
        )
        (input_grad,) = call(
            functools.partial(backward_end, tick),
            "backward_end",
            [piece],
            operands=(g, scaled_grad, saved, norm_gain, stats, swapped(dots)),
            blocks=saved_block,
        )
        if tick + 1 < ticks:
            backward_message = [shifted(input_grad, "segment", -1), cotangents[tick : tick + 1]]
    return (segment_out[None], input_grad[None], gain_total)


def solution(mesh):
    return jax.shard_map(
        shards,
        mesh=mesh,
        in_specs=(
            P("segment", "shard", None),
            P("segment", None, "shard"),
            P("segment", "shard"),
            P("segment", None, "shard"),
            P(None, None, "shard"),
            P("segment", None, "shard"),
            P(None, None, "shard"),
            P("segment", None, None, "shard"),
            P("segment", None, None, "shard"),
            P("segment", None, None, "shard"),
            P(),
            P("segment", None, "shard"),
            P("segment", None, "shard"),
        ),
        out_specs=(P("segment", None, "shard"), P("segment", None, "shard"), P("segment", "shard")),
        check_vma=False,
    )
```

```python
import functools

import jax
import jax.numpy as jnp
from jax import lax
from jax.experimental import pallas as pl
from jax.experimental.pallas import tpu as pltpu
from jax.sharding import PartitionSpec as P

D = 8192
BLOCK = 128
ROWS = 128
WIDTH = 256
SEQ = 64
STATS = 16
RING = 8
HALF = RING * WIDTH
EPSILON = 1e-05
F32 = jnp.float32
BF16 = jnp.bfloat16
VMEM_LIMIT = 20 * 1024 * 1024


def core_pairs():
    return [(index, index ^ 1) for index in range(4 * RING)]


def z_pairs():
    return [(index, index ^ 2) for index in range(4 * RING)]


def near_pairs():
    return [(index, index ^ 4) for index in range(4 * RING)]


def rings():
    return [[4 * y + rest for y in range(RING)] for rest in range(4)]


def half_rings():
    return [[4 * y + rest for y in range(odd, RING, 2)] for odd in range(2) for rest in range(4)]


def swapped(value, groups=None):
    return lax.all_to_all(value, "shard", 0, 0, axis_index_groups=groups, tiled=True)


def shifted(value, axis, steps):
    count = lax.axis_size(axis)
    leading, last = (max(0, -steps), min(count, count - steps))
    return lax.ppermute(value, axis, [(source, source + steps) for source in range(leading, last)])


def call(kernel, name, outs, *, prefetch=(), blocks=None, flops=0, operands=()):
    blocks = blocks or {}

    def spec(position, operand):
        if position in blocks:
            if blocks[position] is None:
                return pl.BlockSpec(memory_space=pl.ANY)
            shape, index_map = blocks[position]
            return pl.BlockSpec(shape, index_map)
        rank = len(operand.shape)
        return pl.BlockSpec(operand.shape, lambda *_: (0,) * rank)

    moved = 0
    for position, operand in enumerate(operands):
        shape = (blocks[position] or ((0,),))[0] if position in blocks else operand.shape
        size = 1
        for length in shape:
            size *= length
        moved += size * operand.dtype.itemsize
    for out in outs:
        moved += out.size * out.dtype.itemsize
    return pl.pallas_call(
        kernel,
        out_shape=outs,
        grid_spec=pltpu.PrefetchScalarGridSpec(
            num_scalar_prefetch=len(prefetch),
            grid=(1,),
            in_specs=[spec(position, operand) for position, operand in enumerate(operands)],
            out_specs=[pl.BlockSpec(out.shape, lambda *_, rank=len(out.shape): (0,) * rank) for out in outs],
        ),
        compiler_params=pltpu.CompilerParams(vmem_limit_bytes=VMEM_LIMIT),
        cost_estimate=pl.CostEstimate(flops=flops, bytes_accessed=moved, transcendentals=0),
        name=name,
    )(*prefetch, *operands)


def shape_of(*dims, dtype=BF16):
    return jax.ShapeDtypeStruct(dims, dtype)


def across(column):
    return jnp.broadcast_to(column, (ROWS, ROWS)).T[0:1]


def down(row):
    square = jnp.broadcast_to(row, (ROWS, ROWS)).T
    return jnp.concatenate([square, square], axis=1)


def split_stats(total):
    high = total.astype(BF16).astype(F32)
    return jnp.concatenate([high, total - high], axis=1).astype(BF16)


def joined_stats(coded):
    value = coded.astype(F32)
    return value[:, :ROWS] + value[:, ROWS:]


def power_row(low, high, sign):
    lane = lax.broadcasted_iota(jnp.int32, (1, WIDTH), 1)
    exponent = sign * jnp.where(lane < BLOCK, low, high)
    magnitude = jnp.abs(exponent)
    grown = jnp.ones((1, WIDTH), F32)
    shrunk = jnp.ones((1, WIDTH), F32)
    for bit in range(4):
        bit_set = (magnitude >> bit) & 1 == 1
        grown = jnp.where(bit_set, grown * 2.0 ** (2**bit), grown)
        shrunk = jnp.where(bit_set, shrunk * 0.5 ** (2**bit), shrunk)
    return jnp.where(exponent < 0, shrunk, grown)


def decoded(message, first_ref, second_ref, exponents, tick):
    low, high = exponents[tick, 0], exponents[tick, 1]
    scale = power_row(low, high, 1)
    inverse = power_row(low, high, -1)
    base = jnp.concatenate([first_ref[0], second_ref[0]], axis=0).astype(F32)
    delta = jnp.clip((message.astype(F32) - base) * inverse, -127.0, 127.0).astype(BF16)
    return (base + delta.astype(F32) * scale).astype(BF16)


def chosen(meta, edge, refs):
    if len(refs) == 1:
        return refs[0][...]
    return jnp.where(meta[0] == edge, refs[1][0].astype(F32), refs[0][...].astype(F32))


def paired(j, odd):
    return 2 * (j % (RING // 2)) + (odd if j < RING // 2 else 1 - odd)


def forward_start(tick, messages, ids, meta, exponents, *refs):
    given, refs = refs[:messages], refs[messages:]
    first, second, gain, weight, x_out, keep, send = refs
    x = decoded(chosen(meta, 0, given), first, second, exponents, tick)
    x_out[...] = x
    x = x.astype(F32)
    scaled = (x * gain[...]).astype(BF16)
    total = across(jnp.sum(x * x, axis=1, keepdims=True))
    stats = split_stats(jnp.broadcast_to(total, (STATS, ROWS)))
    odd, core = meta[1] % 2, meta[3]
    for out, half in ((send, 1 - core), (keep, core)):
        for j in range(RING):
            at = pl.multiple_of((half * RING + paired(j, odd)) * WIDTH, WIDTH)
            part = jnp.dot(scaled, weight[:, pl.ds(at, WIDTH)], preferred_element_type=F32)
            out[j, :ROWS] = part.astype(BF16)
            out[j, ROWS:] = stats


def backward_start(tick, messages, last, ids, meta, exponents, *refs):
    given, (first, second, weight, g_out, keep, send) = refs[:messages], refs[messages:]
    g = decoded(chosen(meta, last, given), first, second, exponents, tick)
    g_out[...] = g
    core = meta[3]
    for out, half in ((send, 1 - core), (keep, core)):
        for j in range(RING):
            at = pl.multiple_of((half * RING + j) * WIDTH, WIDTH)
            part = lax.dot_general(
                g, weight[pl.ds(at, WIDTH), :], (((1,), (1,)), ((), ())), preferred_element_type=F32
            )
            out[j] = part.astype(BF16)


def tall_sum(mine, other, _, *outs):
    stats = split_stats(joined_stats(mine[0, ROWS:]) + joined_stats(other[0, ROWS:]))
    each = outs[0].shape[0]
    for j in range(mine.shape[0]):
        out, at = outs[j // each], j % each
        out[at, :ROWS] = (mine[j, :ROWS].astype(F32) + other[j, :ROWS].astype(F32)).astype(BF16)
        out[at, ROWS:] = stats


def low_sum(mine, other, _, out):
    for j in range(RING):
        out[j] = (mine[j].astype(F32) + other[j].astype(F32)).astype(BF16)


def ring_sum(pieces, out):
    total = pieces[0, :ROWS].astype(F32)
    for j in range(1, pieces.shape[0]):
        total = total + pieces[j, :ROWS].astype(F32)
    out[:ROWS] = total.astype(BF16)
    if out.shape[0] > ROWS:
        stats = joined_stats(pieces[0, ROWS:])
        for j in range(1, pieces.shape[0]):
            stats = stats + joined_stats(pieces[j, ROWS:])
        out[ROWS:] = split_stats(stats)


def forward_share(own, other, out):
    total = joined_stats(own[ROWS:]) + joined_stats(other[ROWS:])
    factor = lax.rsqrt(total[0:1] / D + EPSILON)
    value = own[:ROWS].astype(F32) + other[:ROWS].astype(F32)
    out[...] = jnp.broadcast_to((down(factor) * value).astype(BF16)[None], out.shape)


def backward_share(own, other, out):
    value = (own[...].astype(F32) + other[...].astype(F32)).astype(BF16)
    out[...] = jnp.broadcast_to(value[None], out.shape)


def forward_product(meta, near, far, own_weight, other_weight, mine, others):
    odd, half = meta[1] % 2, RING // 2
    for weight, out in ((other_weight, others), (own_weight, mine)):
        total = jnp.zeros((ROWS, WIDTH), F32)
        for j in range(RING):
            at = pl.multiple_of(paired(j, odd) * WIDTH, WIDTH)
            block = near[j] if j < half else far[j - half]
            total = total + jnp.dot(block, weight[pl.ds(at, WIDTH), :], preferred_element_type=F32)
        out[...] = total


def backward_product(meta, blocks, own_weight, other_weight, mine, others):
    for weight, out in ((other_weight, others), (own_weight, mine)):
        total = jnp.zeros((ROWS, WIDTH), F32)
        for j in range(RING):
            at = j * WIDTH
            total = total + lax.dot_general(
                blocks[j], weight[:, pl.ds(at, WIDTH)], (((1,), (1,)), ((), ())), preferred_element_type=F32
            )
        out[...] = total


def forward_end(x, mine, other, out):
    out[...] = (x[...].astype(F32) + (mine[...] + other[...])).astype(BF16)


def backward_middle(tick, mine, other, saved, gain, scaled_grad, dots):
    value = mine[...] + other[...]
    scaled_grad[...] = value
    terms = [saved[tick].astype(F32) * gain[...] * value]
    if tick == 0:
        for k in range(2):
            kept = saved[k].astype(F32)
            terms.append(kept * kept)
    rows = [across(jnp.sum(term, axis=1, keepdims=True)) for term in terms]
    rows.append(jnp.zeros((8 - len(rows), ROWS), F32))
    dots[...] = jnp.broadcast_to(jnp.concatenate(rows, axis=0)[None], dots.shape)


def backward_end(tick, g, scaled_grad, saved, gain, dots, *refs):
    before, (out, gain_out, *left) = refs[: 2 if tick else 0], refs[2 if tick else 0 :]
    total = dots[0]
    for j in range(1, dots.shape[0]):
        total = total + dots[j]
    if tick == 0:
        squares = total[1:2]
        left[0][...] = jnp.broadcast_to(total[2:3], left[0].shape)
    else:
        squares = before[0][0:1]
    factor = down(lax.rsqrt(squares / D + EPSILON))
    kept = saved[tick].astype(F32)
    sums = jnp.sum(scaled_grad[...] * kept * factor, axis=0, keepdims=True)
    gain_out[...] = sums + before[1][...] if tick else sums
    value = g[...].astype(F32) + factor * gain[...] * scaled_grad[...]
    out[...] = (value - kept * (factor * factor * factor) * down(total[0:1]) / D).astype(BF16)


def forward_scattered(keep, send, after):
    half = shape_of(RING // 2, ROWS + STATS, WIDTH)
    other = lax.ppermute(send, "shard", core_pairs())
    mine, theirs = call(tall_sum, "core_sum", [half, half], operands=(keep, other, after), blocks={2: None})
    other = lax.ppermute(theirs, "shard", near_pairs())
    (pieces,) = call(tall_sum, "near_sum", [half], operands=(mine, other, after), blocks={2: None})
    pieces = swapped(pieces, half_rings())
    (own,) = call(ring_sum, "ring_sum", [shape_of(ROWS + STATS, WIDTH)], operands=(pieces,))
    return own


def backward_scattered(keep, send, after):
    other = lax.ppermute(send, "shard", core_pairs())
    (pieces,) = call(
        low_sum, "low_sum", [shape_of(RING, ROWS, WIDTH)], operands=(keep, other, after), blocks={2: None}
    )
    (own,) = call(ring_sum, "low_ring_sum", [shape_of(ROWS, WIDTH)], operands=(swapped(pieces, rings()),))
    return own, pieces


def over_z(own):
    return lax.ppermute(own, "shard", z_pairs())


def shards(
    value_weight,
    output_weight,
    norm_gain,
    arriving,
    fresh_inputs,
    returning,
    cotangents,
    saved_inputs,
    forward_base,
    backward_base,
    sample_ids,
    forward_exponents,
    backward_exponents,
):
    segment = lax.axis_index("segment")
    segments = lax.axis_size("segment")
    position = lax.axis_index("shard")
    core = position % 2
    meta = jnp.stack([segment, position // 4, position // 2 % 2, core]).astype(jnp.int32)
    value_local, output_local = value_weight[0], output_weight[0]
    saved, ticks = saved_inputs[0], saved_inputs.shape[1]
    half = (1 - core) * HALF
    value_other = lax.ppermute(
        lax.dynamic_slice(value_local, (0, half), (WIDTH, HALF)), "shard", core_pairs()
    )
    output_other = lax.ppermute(
        lax.dynamic_slice(output_local, (half, 0), (HALF, WIDTH)), "shard", core_pairs()
    )
    piece = shape_of(ROWS, WIDTH)
    wide = shape_of(ROWS, WIDTH, dtype=F32)
    start_flops = 2 * ROWS * WIDTH * 2 * HALF

    def base_blocks(first, micro):
        return {
            first + sample: (
                (1, SEQ, WIDTH),
                lambda i, ids, meta, exps, sample=sample: (ids[micro(meta), sample], 0, 0),
            )
            for sample in range(2)
        }

    forward_message, backward_message = [arriving[0]], [returning[0]]
    left = ()
    for tick in range(ticks):
        tall = shape_of(RING, ROWS + STATS, WIDTH)
        count = len(forward_message)
        x, keep, send = call(
            functools.partial(forward_start, tick, count),
            "forward_start",
            [piece, tall, tall],
            prefetch=(sample_ids, meta, forward_exponents[0]),
            operands=(*forward_message, forward_base[0], forward_base[0], norm_gain, value_local),
            blocks=base_blocks(count, lambda meta: tick - meta[0] + segments - 1),
            flops=start_flops,
        )
        low = shape_of(RING, ROWS, WIDTH)
        g, back_keep, back_send = call(
            functools.partial(backward_start, tick, count, segments - 1),
            "backward_start",
            [piece, low, low],
            prefetch=(sample_ids, meta, backward_exponents[0]),
            operands=(*backward_message, backward_base[0], backward_base[0], output_local),
            blocks=base_blocks(count, lambda meta: tick + meta[0]),
            flops=start_flops,
        )
        back_own, pieces = backward_scattered(back_keep, back_send, x if tick == 0 else g)
        own = forward_scattered(keep, send, pieces if tick == 0 else x)

        copies = shape_of(RING // 2, ROWS, WIDTH)
        (pre,) = call(forward_share, "forward_share", [copies], operands=(own, over_z(own)))
        near = swapped(pre, half_rings())
        far = lax.ppermute(near, "shard", near_pairs())
        copies = shape_of(RING, ROWS, WIDTH)
        (value_grad,) = call(
            backward_share, "backward_share", [copies], operands=(back_own, over_z(back_own))
        )
        back_gathered = swapped(value_grad, rings())

        mine, others = call(
            forward_product,
            "forward_product",
            [wide, wide],
            prefetch=(meta,),
            operands=(near, far, output_local, output_other),
            blocks={2: ((HALF, WIDTH), lambda i, meta: (meta[3], 0))},
            flops=start_flops,
        )
        (segment_out,) = call(
            forward_end,
            "forward_end",
            [piece],
            operands=(x, mine, lax.ppermute(others, "shard", core_pairs())),
        )
        if tick + 1 < ticks:
            forward_message = [shifted(segment_out, "segment", 1), fresh_inputs[tick : tick + 1]]

        mine, others = call(
            backward_product,
            "backward_product",
            [wide, wide],
            prefetch=(meta,),
            operands=(back_gathered, value_local, value_other),
            blocks={1: ((WIDTH, HALF), lambda i, meta: (0, meta[3]))},
            flops=start_flops,
        )
        scaled_grad, dots = call(
            functools.partial(backward_middle, tick),
            "backward_middle",
            [wide, shape_of(4 * RING, 8, ROWS, dtype=F32)],
            operands=(mine, lax.ppermute(others, "shard", core_pairs()), saved, norm_gain),
        )
        outs = [piece, shape_of(1, WIDTH, dtype=F32)]
        input_grad, gain_total, *rest = call(
            functools.partial(backward_end, tick),
            "backward_end",
            outs + ([shape_of(8, ROWS, dtype=F32)] if tick == 0 else []),
            operands=(g, scaled_grad, saved, norm_gain, swapped(dots), *left),
        )
        left = (*rest, gain_total)
        if tick + 1 < ticks:
            backward_message = [shifted(input_grad, "segment", -1), cotangents[tick : tick + 1]]
    return (segment_out[None], input_grad[None], gain_total)


def solution(mesh):
    return jax.shard_map(
        shards,
        mesh=mesh,
        in_specs=(
            P("segment", "shard", None),
            P("segment", None, "shard"),
            P("segment", "shard"),
            P("segment", None, "shard"),
            P(None, None, "shard"),
            P("segment", None, "shard"),
            P(None, None, "shard"),
            P("segment", None, None, "shard"),
            P("segment", None, None, "shard"),
            P("segment", None, None, "shard"),
            P(),
            P("segment", None, "shard"),
            P("segment", None, "shard"),
        ),
        out_specs=(P("segment", None, "shard"), P("segment", None, "shard"), P("segment", "shard")),
        check_vma=False,
    )
```

```python
import functools

import jax
import jax.numpy as jnp
from jax import lax
from jax.experimental import pallas as pl
from jax.experimental.pallas import tpu as pltpu
from jax.sharding import PartitionSpec as P

D = 8192
BLOCK = 128
ROWS = 128
WIDTH = 256
SEQ = 64
STATS = 16
RING = 8
HALF = RING * WIDTH
EPSILON = 1e-05
F32 = jnp.float32
BF16 = jnp.bfloat16
VMEM_LIMIT = 20 * 1024 * 1024


def core_pairs():
    return [(index, index ^ 1) for index in range(4 * RING)]


def z_pairs():
    return [(index, index ^ 2) for index in range(4 * RING)]


def rings():
    return [[4 * y + rest for y in range(RING)] for rest in range(4)]


def swapped(value, groups=None):
    return lax.all_to_all(value, "shard", 0, 0, axis_index_groups=groups, tiled=True)


def gate(value, *after):
    return lax.optimization_barrier((value, *after))[0]


def shifted(value, axis, steps):
    count = lax.axis_size(axis)
    leading, last = (max(0, -steps), min(count, count - steps))
    return lax.ppermute(value, axis, [(source, source + steps) for source in range(leading, last)])


def call(kernel, name, outs, *, prefetch=(), blocks=None, operands=(), after=()):
    blocks = blocks or {}
    first, last = len(prefetch) + len(operands), len(prefetch) + len(operands) + len(after)

    def body(*refs):
        kernel(*refs[:first], *refs[last:])

    def spec(position, operand):
        if position in blocks:
            shape, index_map = blocks[position]
            return pl.BlockSpec(shape, index_map)
        rank = len(operand.shape)
        return pl.BlockSpec(operand.shape, lambda *_: (0,) * rank)

    in_specs = [spec(position, operand) for position, operand in enumerate(operands)]
    return pl.pallas_call(
        body,
        out_shape=outs,
        grid_spec=pltpu.PrefetchScalarGridSpec(
            num_scalar_prefetch=len(prefetch),
            grid=(1,),
            in_specs=in_specs + [pl.BlockSpec(memory_space=pl.ANY)] * len(after),
            out_specs=[pl.BlockSpec(out.shape, lambda *_, rank=len(out.shape): (0,) * rank) for out in outs],
        ),
        compiler_params=pltpu.CompilerParams(vmem_limit_bytes=VMEM_LIMIT),
        cost_estimate=pl.CostEstimate(flops=0, bytes_accessed=0, transcendentals=0),
        name=name,
    )(*prefetch, *operands, *after)


def shape_of(*dims, dtype=BF16):
    return jax.ShapeDtypeStruct(dims, dtype)


def across(column):
    return jnp.broadcast_to(column, (ROWS, ROWS)).T[0:1]


def down(row):
    square = jnp.broadcast_to(row, (ROWS, ROWS)).T
    return jnp.concatenate([square, square], axis=1)


def split_stats(total):
    high = total.astype(BF16).astype(F32)
    return jnp.concatenate([high, total - high], axis=1).astype(BF16)


def joined_stats(coded):
    value = coded.astype(F32)
    return value[:, :ROWS] + value[:, ROWS:]


def power_row(low, high, sign):
    lane = lax.broadcasted_iota(jnp.int32, (1, WIDTH), 1)
    exponent = sign * jnp.where(lane < BLOCK, low, high)
    magnitude = jnp.abs(exponent)
    grown = jnp.ones((1, WIDTH), F32)
    shrunk = jnp.ones((1, WIDTH), F32)
    for bit in range(4):
        bit_set = (magnitude >> bit) & 1 == 1
        grown = jnp.where(bit_set, grown * 2.0 ** (2**bit), grown)
        shrunk = jnp.where(bit_set, shrunk * 0.5 ** (2**bit), shrunk)
    return jnp.where(exponent < 0, shrunk, grown)


def decoded(message, first_ref, second_ref, exponents, tick):
    low, high = exponents[tick, 0], exponents[tick, 1]
    scale = power_row(low, high, 1)
    inverse = power_row(low, high, -1)
    base = jnp.concatenate([first_ref[0], second_ref[0]], axis=0).astype(F32)
    delta = jnp.clip((message.astype(F32) - base) * inverse, -127.0, 127.0).astype(BF16)
    return (base + delta.astype(F32) * scale).astype(BF16)


def chosen(meta, edge, refs):
    if len(refs) == 1:
        return refs[0][...]
    return jnp.where(meta[0] == edge, refs[1][0].astype(F32), refs[0][...].astype(F32))


def forward_start(tick, messages, ids, meta, exponents, *refs):
    given, refs = refs[:messages], refs[messages:]
    first, second, gain, weight, x_out, keep, send = refs
    x = decoded(chosen(meta, 0, given), first, second, exponents, tick)
    x_out[...] = x
    x = x.astype(F32)
    scaled = (x * gain[...]).astype(BF16)
    total = across(jnp.sum(x * x, axis=1, keepdims=True))
    stats = split_stats(jnp.broadcast_to(total, (STATS, ROWS)))
    core = meta[3]
    for out, half in ((send, 1 - core), (keep, core)):
        for j in range(RING):
            at = pl.multiple_of((half * RING + j) * WIDTH, WIDTH)
            part = jnp.dot(scaled, weight[:, pl.ds(at, WIDTH)], preferred_element_type=F32)
            out[j, :ROWS] = part.astype(BF16)
            out[j, ROWS:] = stats


def backward_start(tick, messages, last, ids, meta, exponents, *refs):
    given, (first, second, weight, g_out, keep, send) = refs[:messages], refs[messages:]
    g = decoded(chosen(meta, last, given), first, second, exponents, tick)
    g_out[...] = g
    core = meta[3]
    for out, half in ((send, 1 - core), (keep, core)):
        for j in range(RING):
            at = pl.multiple_of((half * RING + j) * WIDTH, WIDTH)
            part = lax.dot_general(
                g, weight[pl.ds(at, WIDTH), :], (((1,), (1,)), ((), ())), preferred_element_type=F32
            )
            out[j] = part.astype(BF16)


def core_sum(mine, other, out):
    for j in range(RING):
        out[j, :ROWS] = (mine[j, :ROWS].astype(F32) + other[j, :ROWS].astype(F32)).astype(BF16)
    if out.shape[1] > ROWS:
        stats = split_stats(joined_stats(mine[0, ROWS:]) + joined_stats(other[0, ROWS:]))
        for j in range(RING):
            out[j, ROWS:] = stats


def ring_sum(pieces, out):
    total = pieces[0, :ROWS].astype(F32)
    for j in range(1, pieces.shape[0]):
        total = total + pieces[j, :ROWS].astype(F32)
    out[:ROWS] = total.astype(BF16)
    if out.shape[0] > ROWS:
        stats = joined_stats(pieces[0, ROWS:])
        for j in range(1, pieces.shape[0]):
            stats = stats + joined_stats(pieces[j, ROWS:])
        out[ROWS:] = split_stats(stats)


def forward_share(own, other, out):
    total = joined_stats(own[ROWS:]) + joined_stats(other[ROWS:])
    factor = lax.rsqrt(total[0:1] / D + EPSILON)
    value = own[:ROWS].astype(F32) + other[:ROWS].astype(F32)
    out[...] = jnp.broadcast_to((down(factor) * value).astype(BF16)[None], out.shape)


def backward_share(own, other, out):
    value = (own[...].astype(F32) + other[...].astype(F32)).astype(BF16)
    out[...] = jnp.broadcast_to(value[None], out.shape)


def halves(value, output, value_out, output_out):
    value_out[...] = value[...]
    output_out[...] = output[...]


def forward_product(blocks, own_weight, other_weight, mine, others):
    for weight, out in ((other_weight, others), (own_weight, mine)):
        total = jnp.zeros((ROWS, WIDTH), F32)
        for j in range(RING):
            rows = weight[j * WIDTH : (j + 1) * WIDTH, :]
            total = total + jnp.dot(blocks[j], rows, preferred_element_type=F32)
        out[...] = total


def backward_product(blocks, own_weight, other_weight, mine, others):
    for weight, out in ((other_weight, others), (own_weight, mine)):
        total = jnp.zeros((ROWS, WIDTH), F32)
        for j in range(RING):
            columns = weight[:, j * WIDTH : (j + 1) * WIDTH]
            total = total + lax.dot_general(
                blocks[j], columns, (((1,), (1,)), ((), ())), preferred_element_type=F32
            )
        out[...] = total


def forward_end(x, mine, other, out):
    out[...] = (x[...].astype(F32) + (mine[...] + other[...])).astype(BF16)


def backward_middle(tick, mine, other, saved, gain, scaled_grad, dots):
    value = mine[...] + other[...]
    scaled_grad[...] = value
    terms = [saved[tick].astype(F32) * gain[...] * value]
    if tick == 0:
        for k in range(2):
            kept = saved[k].astype(F32)
            terms.append(kept * kept)
    rows = [across(jnp.sum(term, axis=1, keepdims=True)) for term in terms]
    rows.append(jnp.zeros((8 - len(rows), ROWS), F32))
    dots[...] = jnp.broadcast_to(jnp.concatenate(rows, axis=0)[None], dots.shape)


def backward_end(tick, g, scaled_grad, saved, gain, dots, *refs):
    before, (out, gain_out, *left) = refs[: 2 if tick else 0], refs[2 if tick else 0 :]
    total = dots[0]
    for j in range(1, dots.shape[0]):
        total = total + dots[j]
    if tick == 0:
        squares = total[1:2]
        left[0][...] = jnp.broadcast_to(total[2:3], left[0].shape)
    else:
        squares = before[0][0:1]
    factor = down(lax.rsqrt(squares / D + EPSILON))
    kept = saved[tick].astype(F32)
    sums = jnp.sum(scaled_grad[...] * kept * factor, axis=0, keepdims=True)
    gain_out[...] = sums + before[1][...] if tick else sums
    value = g[...].astype(F32) + factor * gain[...] * scaled_grad[...]
    out[...] = (value - kept * (factor * factor * factor) * down(total[0:1]) / D).astype(BF16)


def over(value, pairs):
    return lax.ppermute(value, "shard", pairs)


def shards(
    value_weight,
    output_weight,
    norm_gain,
    arriving,
    fresh_inputs,
    returning,
    cotangents,
    saved_inputs,
    forward_base,
    backward_base,
    sample_ids,
    forward_exponents,
    backward_exponents,
):
    segment = lax.axis_index("segment")
    segments = lax.axis_size("segment")
    position = lax.axis_index("shard")
    core = position % 2
    meta = jnp.stack([segment, position // 4, position // 2 % 2, core]).astype(jnp.int32)
    value_local, output_local = value_weight[0], output_weight[0]
    saved = saved_inputs[0]
    low = shape_of(ROWS, WIDTH)
    wide = shape_of(ROWS, WIDTH, dtype=F32)
    tall = shape_of(ROWS + STATS, WIDTH)
    eight = shape_of(RING, ROWS, WIDTH)
    eight_tall = shape_of(RING, ROWS + STATS, WIDTH)
    row = shape_of(1, WIDTH, dtype=F32)
    own_half = {1: ((HALF, WIDTH), lambda i, meta: (meta[3], 0))}
    own_columns = {1: ((WIDTH, HALF), lambda i, meta: (0, meta[3]))}

    def base_blocks(first, micro):
        return {
            first + sample: (
                (1, SEQ, WIDTH),
                lambda i, ids, meta, exps, sample=sample: (ids[micro(meta), sample], 0, 0),
            )
            for sample in range(2)
        }

    def forward_begin(tick, messages, *after):
        count = len(messages)
        x, keep, send = call(
            functools.partial(forward_start, tick, count),
            "forward_start",
            [low, eight_tall, eight_tall],
            prefetch=(sample_ids, meta, forward_exponents[0]),
            operands=(*messages, forward_base[0], forward_base[0], norm_gain, value_local),
            blocks=base_blocks(count, lambda meta: tick - meta[0] + segments - 1),
            after=after,
        )
        operands = (keep, over(send, core_pairs()))
        return x, *call(core_sum, "forward_core_sum", [eight_tall], operands=operands)

    def backward_begin(tick, messages, *after):
        count = len(messages)
        g, keep, send = call(
            functools.partial(backward_start, tick, count, segments - 1),
            "backward_start",
            [low, eight, eight],
            prefetch=(sample_ids, meta, backward_exponents[0]),
            operands=(*messages, backward_base[0], backward_base[0], output_local),
            blocks=base_blocks(count, lambda meta: tick + meta[0]),
            after=after,
        )
        operands = (keep, over(send, core_pairs()))
        return g, *call(core_sum, "backward_core_sum", [eight], operands=operands)

    def forward_turn(pieces, *after):
        (own,) = call(ring_sum, "forward_ring_sum", [tall], operands=(pieces,), after=after)
        return call(forward_share, "forward_share", [eight], operands=(own, over(own, z_pairs())))[0]

    def backward_turn(pieces, *after):
        (own,) = call(ring_sum, "backward_ring_sum", [low], operands=(pieces,), after=after)
        return call(backward_share, "backward_share", [eight], operands=(own, over(own, z_pairs())))[0]

    def with_meta(kernel):
        return lambda _, *refs: kernel(*refs)

    def forward_finish(x, gathered, *after):
        mine, others = call(
            with_meta(forward_product),
            "forward_product",
            [wide, wide],
            prefetch=(meta,),
            operands=(gathered, output_local, output_other),
            blocks=own_half,
            after=after,
        )
        operands = (x, mine, over(others, core_pairs()))
        return call(forward_end, "forward_end", [low], operands=operands)[0]

    def backward_dots(tick, gathered, *after):
        mine, others = call(
            with_meta(backward_product),
            "backward_product",
            [wide, wide],
            prefetch=(meta,),
            operands=(gathered, value_local, value_other),
            blocks=own_columns,
            after=after,
        )
        return call(
            functools.partial(backward_middle, tick),
            "backward_middle",
            [wide, shape_of(4 * RING, 8, ROWS, dtype=F32)],
            operands=(mine, over(others, core_pairs()), saved, norm_gain),
        )

    def backward_finish(tick, g, scaled_grad, dots, left, *after):
        return call(
            functools.partial(backward_end, tick),
            "backward_end",
            [low, row] + ([shape_of(8, ROWS, dtype=F32)] if tick == 0 else []),
            operands=(g, scaled_grad, saved, norm_gain, dots, *left),
            after=after,
        )

    g, back_pieces = backward_begin(0, [returning[0]])
    gated = gate(back_pieces)
    back_landed = swapped(gated, rings())

    x, pieces = forward_begin(0, [arriving[0]], gated)
    value_half, output_half = call(
        with_meta(halves),
        "halves",
        [shape_of(WIDTH, HALF), shape_of(HALF, WIDTH)],
        prefetch=(meta,),
        operands=(value_local, output_local),
        blocks={
            0: ((WIDTH, HALF), lambda i, meta: (0, 1 - meta[3])),
            1: ((HALF, WIDTH), lambda i, meta: (1 - meta[3], 0)),
        },
        after=(gated,),
    )
    value_other, output_other = over(value_half, core_pairs()), over(output_half, core_pairs())
    gated = gate(pieces, back_landed, value_other, output_other)
    landed = swapped(gated, rings())

    copies = backward_turn(back_landed, gated)
    gated = gate(copies, landed)
    back_gathered = swapped(gated, rings())

    copies = forward_turn(landed, gated)
    gated = gate(copies, back_gathered)
    gathered = swapped(gated, rings())

    scaled_grad, dots = backward_dots(0, back_gathered, gated)
    gated = gate(dots, gathered)
    all_dots = swapped(gated)

    segment_out = forward_finish(x, gathered, gated)
    x, pieces = forward_begin(1, [shifted(segment_out, "segment", 1), fresh_inputs])
    gated = gate(pieces, all_dots)
    landed = swapped(gated, rings())

    input_grad, gain_total, squares = backward_finish(0, g, scaled_grad, all_dots, (), gated)
    g, back_pieces = backward_begin(1, [shifted(input_grad, "segment", -1), cotangents])
    gated = gate(back_pieces, landed)
    back_landed = swapped(gated, rings())

    copies = forward_turn(landed, gated)
    gated = gate(copies, back_landed)
    gathered = swapped(gated, rings())

    copies = backward_turn(back_landed, gated)
    gated = gate(copies, gathered)
    back_gathered = swapped(gated, rings())

    segment_out = forward_finish(x, gathered, gated)
    scaled_grad, dots = backward_dots(1, back_gathered, segment_out)
    all_dots = swapped(dots)
    input_grad, gain_total = backward_finish(1, g, scaled_grad, all_dots, (squares, gain_total))
    return (segment_out[None], input_grad[None], gain_total)


def solution(mesh):
    return jax.shard_map(
        shards,
        mesh=mesh,
        in_specs=(
            P("segment", "shard", None),
            P("segment", None, "shard"),
            P("segment", "shard"),
            P("segment", None, "shard"),
            P(None, None, "shard"),
            P("segment", None, "shard"),
            P(None, None, "shard"),
            P("segment", None, None, "shard"),
            P("segment", None, None, "shard"),
            P("segment", None, None, "shard"),
            P(),
            P("segment", None, "shard"),
            P("segment", None, "shard"),
        ),
        out_specs=(P("segment", None, "shard"), P("segment", None, "shard"), P("segment", "shard")),
        check_vma=False,
    )
```

```python
import functools

import jax
import jax.numpy as jnp
from jax import lax
from jax.experimental import pallas as pl
from jax.experimental.pallas import tpu as pltpu
from jax.sharding import PartitionSpec as P

D = 8192
BLOCK = 128
ROWS = 128
WIDTH = 256
SEQ = 64
STATS = 16
RING = 8
HALF = RING * WIDTH
EPSILON = 1e-05
F32 = jnp.float32
BF16 = jnp.bfloat16
VMEM_LIMIT = 20 * 1024 * 1024
WIDE_LIMIT = 56 * 1024 * 1024
DOT_ROWS = 16


def core_pairs():
    return [(index, index ^ 1) for index in range(4 * RING)]


def z_pairs():
    return [(index, index ^ 2) for index in range(4 * RING)]


def rings():
    return [[4 * y + rest for y in range(RING)] for rest in range(4)]


def swapped(value, groups=None):
    return lax.all_to_all(value, "shard", 0, 0, axis_index_groups=groups, tiled=True)


def gate(value, *after):
    return lax.optimization_barrier((value, *after))[0]


def shifted(value, axis, steps):
    count = lax.axis_size(axis)
    leading, last = (max(0, -steps), min(count, count - steps))
    return lax.ppermute(value, axis, [(source, source + steps) for source in range(leading, last)])


def call(kernel, name, outs, *, prefetch=(), blocks=None, operands=(), after=(), limit=VMEM_LIMIT):
    blocks = blocks or {}
    first, last = len(prefetch) + len(operands), len(prefetch) + len(operands) + len(after)

    def body(*refs):
        kernel(*refs[:first], *refs[last:])

    def spec(position, operand):
        if position in blocks:
            shape, index_map = blocks[position]
            return pl.BlockSpec(shape, index_map)
        rank = len(operand.shape)
        return pl.BlockSpec(operand.shape, lambda *_: (0,) * rank)

    in_specs = [spec(position, operand) for position, operand in enumerate(operands)]
    return pl.pallas_call(
        body,
        out_shape=outs,
        grid_spec=pltpu.PrefetchScalarGridSpec(
            num_scalar_prefetch=len(prefetch),
            grid=(1,),
            in_specs=in_specs + [pl.BlockSpec(memory_space=pl.ANY)] * len(after),
            out_specs=[pl.BlockSpec(out.shape, lambda *_, rank=len(out.shape): (0,) * rank) for out in outs],
        ),
        compiler_params=pltpu.CompilerParams(vmem_limit_bytes=limit),
        cost_estimate=pl.CostEstimate(flops=0, bytes_accessed=0, transcendentals=0),
        name=name,
    )(*prefetch, *operands, *after)


def shape_of(*dims, dtype=BF16):
    return jax.ShapeDtypeStruct(dims, dtype)


def across(column):
    return jnp.broadcast_to(column, (ROWS, ROWS)).T[0:1]


def down(row):
    square = jnp.broadcast_to(row, (ROWS, ROWS)).T
    return jnp.concatenate([square, square], axis=1)


def split_stats(total):
    high = total.astype(BF16).astype(F32)
    return jnp.concatenate([high, total - high], axis=1).astype(BF16)


def joined_stats(coded):
    value = coded.astype(F32)
    return value[:, :ROWS] + value[:, ROWS:]


def power_row(low, high, sign):
    lane = lax.broadcasted_iota(jnp.int32, (1, WIDTH), 1)
    exponent = sign * jnp.where(lane < BLOCK, low, high)
    magnitude = jnp.abs(exponent)
    grown = jnp.ones((1, WIDTH), F32)
    shrunk = jnp.ones((1, WIDTH), F32)
    for bit in range(4):
        bit_set = (magnitude >> bit) & 1 == 1
        grown = jnp.where(bit_set, grown * 2.0 ** (2**bit), grown)
        shrunk = jnp.where(bit_set, shrunk * 0.5 ** (2**bit), shrunk)
    return jnp.where(exponent < 0, shrunk, grown)


def decoded(message, first_ref, second_ref, exponents, tick):
    low, high = exponents[tick, 0], exponents[tick, 1]
    scale = power_row(low, high, 1)
    inverse = power_row(low, high, -1)
    base = jnp.concatenate([first_ref[0], second_ref[0]], axis=0).astype(F32)
    delta = jnp.clip((message.astype(F32) - base) * inverse, -127.0, 127.0).astype(BF16)
    return (base + delta.astype(F32) * scale).astype(BF16)


def chosen(meta, edge, refs):
    if len(refs) == 1:
        return refs[0][...]
    return jnp.where(meta[0] == edge, refs[1][0].astype(F32), refs[0][...].astype(F32))


def forward_start(tick, messages, ids, meta, exponents, *refs):
    given, refs = refs[:messages], refs[messages:]
    first, second, gain, weight, x_out, keep, send = refs
    x = decoded(chosen(meta, 0, given), first, second, exponents, tick)
    x_out[...] = x
    x = x.astype(F32)
    scaled = (x * gain[...]).astype(BF16)
    total = across(jnp.sum(x * x, axis=1, keepdims=True))
    stats = split_stats(jnp.broadcast_to(total, (STATS, ROWS)))
    core = meta[3]
    for out, half in ((send, 1 - core), (keep, core)):
        for j in range(RING):
            at = pl.multiple_of((half * RING + j) * WIDTH, WIDTH)
            part = jnp.dot(scaled, weight[:, pl.ds(at, WIDTH)], preferred_element_type=F32)
            out[j, :ROWS] = part.astype(BF16)
            out[j, ROWS:] = stats


def backward_start(tick, messages, last, ids, meta, exponents, *refs):
    given, (first, second, weight, g_out, keep, send) = refs[:messages], refs[messages:]
    g = decoded(chosen(meta, last, given), first, second, exponents, tick)
    g_out[...] = g
    core = meta[3]
    for out, half in ((send, 1 - core), (keep, core)):
        for j in range(RING):
            at = pl.multiple_of((half * RING + j) * WIDTH, WIDTH)
            part = lax.dot_general(
                g, weight[pl.ds(at, WIDTH), :], (((1,), (1,)), ((), ())), preferred_element_type=F32
            )
            out[j] = part.astype(BF16)


def core_sum(mine, other, out):
    for j in range(RING):
        out[j, :ROWS] = (mine[j, :ROWS].astype(F32) + other[j, :ROWS].astype(F32)).astype(BF16)
    if out.shape[1] > ROWS:
        stats = split_stats(joined_stats(mine[0, ROWS:]) + joined_stats(other[0, ROWS:]))
        for j in range(RING):
            out[j, ROWS:] = stats


def ring_sum(pieces, out):
    total = pieces[0, :ROWS].astype(F32)
    for j in range(1, pieces.shape[0]):
        total = total + pieces[j, :ROWS].astype(F32)
    out[:ROWS] = total.astype(BF16)
    if out.shape[0] > ROWS:
        stats = joined_stats(pieces[0, ROWS:])
        for j in range(1, pieces.shape[0]):
            stats = stats + joined_stats(pieces[j, ROWS:])
        out[ROWS:] = split_stats(stats)


def forward_share(own, other, out):
    total = joined_stats(own[ROWS:]) + joined_stats(other[ROWS:])
    factor = lax.rsqrt(total[0:1] / D + EPSILON)
    value = own[:ROWS].astype(F32) + other[:ROWS].astype(F32)
    out[...] = jnp.broadcast_to((down(factor) * value).astype(BF16)[None], out.shape)


def backward_share(own, other, out):
    value = (own[...].astype(F32) + other[...].astype(F32)).astype(BF16)
    out[...] = jnp.broadcast_to(value[None], out.shape)


def half(weight, out):
    out[...] = weight[...]


def forward_product(blocks, own_weight, other_weight, mine, others):
    for weight, out in ((other_weight, others), (own_weight, mine)):
        total = jnp.zeros((ROWS, WIDTH), F32)
        for j in range(RING):
            rows = weight[j * WIDTH : (j + 1) * WIDTH, :]
            total = total + jnp.dot(blocks[j], rows, preferred_element_type=F32)
        out[...] = total


def backward_product(blocks, own_weight, other_weight, mine, others):
    for weight, out in ((other_weight, others), (own_weight, mine)):
        total = jnp.zeros((ROWS, WIDTH), F32)
        for j in range(RING):
            columns = weight[:, j * WIDTH : (j + 1) * WIDTH]
            total = total + lax.dot_general(
                blocks[j], columns, (((1,), (1,)), ((), ())), preferred_element_type=F32
            )
        out[...] = total


def forward_end(x, mine, other, out):
    out[...] = (x[...].astype(F32) + (mine[...] + other[...])).astype(BF16)


def backward_middle(tick, mine, other, saved, gain, scaled_grad, dots):
    value = mine[...] + other[...]
    scaled_grad[...] = value
    terms = [saved[tick].astype(F32) * gain[...] * value]
    if tick == 0:
        for k in range(2):
            kept = saved[k].astype(F32)
            terms.append(kept * kept)
    rows = [across(jnp.sum(term, axis=1, keepdims=True)) for term in terms]
    rows.append(jnp.zeros((DOT_ROWS - len(rows), ROWS), F32))
    dots[...] = jnp.broadcast_to(jnp.concatenate(rows, axis=0)[None], dots.shape)


def backward_end(tick, g, scaled_grad, saved, gain, dots, *refs):
    before, (out, gain_out, *left) = refs[: 2 if tick else 0], refs[2 if tick else 0 :]
    total = dots[0, :8]
    for j in range(1, dots.shape[0]):
        total = total + dots[j, :8]
    if tick == 0:
        squares = total[1:2]
        left[0][...] = jnp.broadcast_to(total[2:3], left[0].shape)
    else:
        squares = before[0][0:1]
    factor = down(lax.rsqrt(squares / D + EPSILON))
    kept = saved[tick].astype(F32)
    sums = jnp.sum(scaled_grad[...] * kept * factor, axis=0, keepdims=True)
    gain_out[...] = sums + before[1][...] if tick else sums
    value = g[...].astype(F32) + factor * gain[...] * scaled_grad[...]
    out[...] = (value - kept * (factor * factor * factor) * down(total[0:1]) / D).astype(BF16)


def over(value, pairs):
    return lax.ppermute(value, "shard", pairs)


def shards(
    value_weight,
    output_weight,
    norm_gain,
    arriving,
    fresh_inputs,
    returning,
    cotangents,
    saved_inputs,
    forward_base,
    backward_base,
    sample_ids,
    forward_exponents,
    backward_exponents,
):
    segment = lax.axis_index("segment")
    segments = lax.axis_size("segment")
    position = lax.axis_index("shard")
    core = position % 2
    meta = jnp.stack([segment, position // 4, position // 2 % 2, core]).astype(jnp.int32)
    value_local, output_local = value_weight[0], output_weight[0]
    saved = saved_inputs[0]
    low = shape_of(ROWS, WIDTH)
    wide = shape_of(ROWS, WIDTH, dtype=F32)
    tall = shape_of(ROWS + STATS, WIDTH)
    eight = shape_of(RING, ROWS, WIDTH)
    eight_tall = shape_of(RING, ROWS + STATS, WIDTH)
    row = shape_of(1, WIDTH, dtype=F32)
    own_half = {1: ((HALF, WIDTH), lambda i, meta: (meta[3], 0))}
    own_columns = {1: ((WIDTH, HALF), lambda i, meta: (0, meta[3]))}

    def base_blocks(first, micro):
        return {
            first + sample: (
                (1, SEQ, WIDTH),
                lambda i, ids, meta, exps, sample=sample: (ids[micro(meta), sample], 0, 0),
            )
            for sample in range(2)
        }

    def forward_begin(tick, messages, *after):
        count = len(messages)
        x, keep, send = call(
            functools.partial(forward_start, tick, count),
            "forward_start",
            [low, eight_tall, eight_tall],
            prefetch=(sample_ids, meta, forward_exponents[0]),
            operands=(*messages, forward_base[0], forward_base[0], norm_gain, value_local),
            blocks=base_blocks(count, lambda meta: tick - meta[0] + segments - 1),
            after=after,
        )
        operands = (keep, over(send, core_pairs()))
        return x, *call(core_sum, "forward_core_sum", [eight_tall], operands=operands)

    def backward_begin(tick, messages, *after):
        count = len(messages)
        g, keep, send = call(
            functools.partial(backward_start, tick, count, segments - 1),
            "backward_start",
            [low, eight, eight],
            prefetch=(sample_ids, meta, backward_exponents[0]),
            operands=(*messages, backward_base[0], backward_base[0], output_local),
            blocks=base_blocks(count, lambda meta: tick + meta[0]),
            after=after,
            limit=VMEM_LIMIT if tick else WIDE_LIMIT,
        )
        operands = (keep, over(send, core_pairs()))
        return g, *call(core_sum, "backward_core_sum", [eight], operands=operands)

    def forward_turn(pieces, *after):
        (own,) = call(ring_sum, "forward_ring_sum", [tall], operands=(pieces,), after=after)
        return call(forward_share, "forward_share", [eight], operands=(own, over(own, z_pairs())))[0]

    def backward_turn(pieces, *after):
        (own,) = call(ring_sum, "backward_ring_sum", [low], operands=(pieces,), after=after)
        return call(backward_share, "backward_share", [eight], operands=(own, over(own, z_pairs())))[0]

    def with_meta(kernel):
        return lambda _, *refs: kernel(*refs)

    def exchanged_half(weight, block, index_map, *after):
        (own,) = call(
            with_meta(half),
            "half",
            [shape_of(*block)],
            prefetch=(meta,),
            operands=(weight,),
            blocks={0: (block, index_map)},
            after=after,
        )
        return over(own, core_pairs())

    def forward_finish(x, gathered, *after):
        mine, others = call(
            with_meta(forward_product),
            "forward_product",
            [wide, wide],
            prefetch=(meta,),
            operands=(gathered, output_local, output_other),
            blocks=own_half,
            after=after,
        )
        operands = (x, mine, over(others, core_pairs()))
        return call(forward_end, "forward_end", [low], operands=operands)[0]

    def backward_dots(tick, gathered, *after):
        mine, others = call(
            with_meta(backward_product),
            "backward_product",
            [wide, wide],
            prefetch=(meta,),
            operands=(gathered, value_local, value_other),
            blocks=own_columns,
            after=after,
            limit=WIDE_LIMIT if tick else VMEM_LIMIT,
        )
        return call(
            functools.partial(backward_middle, tick),
            "backward_middle",
            [wide, shape_of(4 * RING, DOT_ROWS, ROWS, dtype=F32)],
            operands=(mine, over(others, core_pairs()), saved, norm_gain),
        )

    def backward_finish(tick, g, scaled_grad, dots, left, *after):
        return call(
            functools.partial(backward_end, tick),
            "backward_end",
            [low, row] + ([shape_of(8, ROWS, dtype=F32)] if tick == 0 else []),
            operands=(g, scaled_grad, saved, norm_gain, dots, *left),
            after=after,
        )

    g, back_pieces = backward_begin(0, [returning[0]])
    gated = gate(back_pieces)
    back_landed = swapped(gated, rings())

    x, pieces = forward_begin(0, [arriving[0]], gated)
    gated = gate(pieces, back_landed)
    landed = swapped(gated, rings())

    value_other = exchanged_half(value_local, (WIDTH, HALF), lambda i, meta: (0, 1 - meta[3]), gated)
    copies = backward_turn(back_landed, gated)
    gated = gate(copies, landed, value_other)
    back_gathered = swapped(gated, rings())

    output_other = exchanged_half(output_local, (HALF, WIDTH), lambda i, meta: (1 - meta[3], 0), gated)
    copies = forward_turn(landed, gated)
    gated = gate(copies, back_gathered, output_other)
    gathered = swapped(gated, rings())

    scaled_grad, dots = backward_dots(0, back_gathered, gated)
    gated = gate(dots, gathered)
    all_dots = swapped(gated)

    segment_out = forward_finish(x, gathered, gated)
    x, pieces = forward_begin(1, [shifted(segment_out, "segment", 1), fresh_inputs])
    gated = gate(pieces, all_dots)
    landed = swapped(gated, rings())

    input_grad, gain_total, squares = backward_finish(0, g, scaled_grad, all_dots, (), gated)
    g, back_pieces = backward_begin(1, [shifted(input_grad, "segment", -1), cotangents])
    gated = gate(back_pieces, landed)
    back_landed = swapped(gated, rings())

    copies = forward_turn(landed, gated)
    gated = gate(copies, back_landed)
    gathered = swapped(gated, rings())

    copies = backward_turn(back_landed, gated)
    gated = gate(copies, gathered)
    back_gathered = swapped(gated, rings())

    segment_out = forward_finish(x, gathered, gated)
    scaled_grad, dots = backward_dots(1, back_gathered, segment_out)
    all_dots = swapped(dots)
    input_grad, gain_total = backward_finish(1, g, scaled_grad, all_dots, (squares, gain_total))
    return (segment_out[None], input_grad[None], gain_total)


def solution(mesh):
    return jax.shard_map(
        shards,
        mesh=mesh,
        in_specs=(
            P("segment", "shard", None),
            P("segment", None, "shard"),
            P("segment", "shard"),
            P("segment", None, "shard"),
            P(None, None, "shard"),
            P("segment", None, "shard"),
            P(None, None, "shard"),
            P("segment", None, None, "shard"),
            P("segment", None, None, "shard"),
            P("segment", None, None, "shard"),
            P(),
            P("segment", None, "shard"),
            P("segment", None, "shard"),
        ),
        out_specs=(P("segment", None, "shard"), P("segment", None, "shard"), P("segment", "shard")),
        check_vma=False,
    )
```

```python
import functools

import jax
import jax.numpy as jnp
from jax import lax
from jax.experimental import pallas as pl
from jax.experimental.pallas import tpu as pltpu
from jax.sharding import PartitionSpec as P

D = 8192
BLOCK = 128
ROWS = 128
WIDTH = 256
SEQ = 64
STATS = 16
RING = 8
HALF = RING * WIDTH
EPSILON = 1e-05
F32 = jnp.float32
BF16 = jnp.bfloat16
VMEM_LIMIT = 20 * 1024 * 1024
DOT_ROWS = 8


def core_pairs():
    return [(index, index ^ 1) for index in range(4 * RING)]


def z_pairs():
    return [(index, index ^ 2) for index in range(4 * RING)]


def rings():
    return [[4 * y + rest for y in range(RING)] for rest in range(4)]


def swapped(value, groups=None):
    return lax.all_to_all(value, "shard", 0, 0, axis_index_groups=groups, tiled=True)


def gate(value, *after):
    return lax.optimization_barrier((value, *after))[0]


def shifted(value, axis, steps):
    count = lax.axis_size(axis)
    leading, last = (max(0, -steps), min(count, count - steps))
    return lax.ppermute(value, axis, [(source, source + steps) for source in range(leading, last)])


def call(kernel, name, outs, *, prefetch=(), blocks=None, operands=(), after=()):
    blocks = blocks or {}
    first, last = len(prefetch) + len(operands), len(prefetch) + len(operands) + len(after)

    def body(*refs):
        kernel(*refs[:first], *refs[last:])

    def spec(position, operand):
        if position in blocks:
            shape, index_map = blocks[position]
            return pl.BlockSpec(shape, index_map)
        rank = len(operand.shape)
        return pl.BlockSpec(operand.shape, lambda *_: (0,) * rank)

    in_specs = [spec(position, operand) for position, operand in enumerate(operands)]
    return pl.pallas_call(
        body,
        out_shape=outs,
        grid_spec=pltpu.PrefetchScalarGridSpec(
            num_scalar_prefetch=len(prefetch),
            grid=(1,),
            in_specs=in_specs + [pl.BlockSpec(memory_space=pl.ANY)] * len(after),
            out_specs=[pl.BlockSpec(out.shape, lambda *_, rank=len(out.shape): (0,) * rank) for out in outs],
        ),
        compiler_params=pltpu.CompilerParams(vmem_limit_bytes=VMEM_LIMIT),
        cost_estimate=pl.CostEstimate(flops=0, bytes_accessed=0, transcendentals=0),
        name=name,
    )(*prefetch, *operands, *after)


def shape_of(*dims, dtype=BF16):
    return jax.ShapeDtypeStruct(dims, dtype)


def across(column):
    return jnp.broadcast_to(column, (ROWS, ROWS)).T[0:1]


def down(row):
    square = jnp.broadcast_to(row, (ROWS, ROWS)).T
    return jnp.concatenate([square, square], axis=1)


def split_stats(total):
    high = total.astype(BF16).astype(F32)
    return jnp.concatenate([high, total - high], axis=1).astype(BF16)


def joined_stats(coded):
    value = coded.astype(F32)
    return value[:, :ROWS] + value[:, ROWS:]


def power_row(low, high, sign):
    lane = lax.broadcasted_iota(jnp.int32, (1, WIDTH), 1)
    exponent = sign * jnp.where(lane < BLOCK, low, high)
    magnitude = jnp.abs(exponent)
    grown = jnp.ones((1, WIDTH), F32)
    shrunk = jnp.ones((1, WIDTH), F32)
    for bit in range(4):
        bit_set = (magnitude >> bit) & 1 == 1
        grown = jnp.where(bit_set, grown * 2.0 ** (2**bit), grown)
        shrunk = jnp.where(bit_set, shrunk * 0.5 ** (2**bit), shrunk)
    return jnp.where(exponent < 0, shrunk, grown)


def decoded(message, first_ref, second_ref, exponents, tick):
    low, high = exponents[tick, 0], exponents[tick, 1]
    scale = power_row(low, high, 1)
    inverse = power_row(low, high, -1)
    base = jnp.concatenate([first_ref[0], second_ref[0]], axis=0).astype(F32)
    delta = jnp.clip((message.astype(F32) - base) * inverse, -127.0, 127.0).astype(BF16)
    return (base + delta.astype(F32) * scale).astype(BF16)


def chosen(meta, edge, refs):
    if len(refs) == 1:
        return refs[0][...]
    return jnp.where(meta[0] == edge, refs[1][0].astype(F32), refs[0][...].astype(F32))


def forward_start(tick, messages, ids, meta, exponents, *refs):
    given, refs = refs[:messages], refs[messages:]
    first, second, gain, weight, x_out, keep, send = refs
    x = decoded(chosen(meta, 0, given), first, second, exponents, tick)
    x_out[...] = x
    x = x.astype(F32)
    scaled = (x * gain[...]).astype(BF16)
    total = across(jnp.sum(x * x, axis=1, keepdims=True))
    stats = split_stats(jnp.broadcast_to(total, (STATS, ROWS)))
    core = meta[3]
    for out, half in ((send, 1 - core), (keep, core)):
        for j in range(RING):
            at = pl.multiple_of((half * RING + j) * WIDTH, WIDTH)
            part = jnp.dot(scaled, weight[:, pl.ds(at, WIDTH)], preferred_element_type=F32)
            out[j, :ROWS] = part.astype(BF16)
            out[j, ROWS:] = stats


def backward_start(tick, messages, last, ids, meta, exponents, *refs):
    given, (first, second, weight, g_out, keep, send) = refs[:messages], refs[messages:]
    g = decoded(chosen(meta, last, given), first, second, exponents, tick)
    g_out[...] = g
    core = meta[3]
    for out, half in ((send, 1 - core), (keep, core)):
        for j in range(RING):
            at = pl.multiple_of((half * RING + j) * WIDTH, WIDTH)
            part = lax.dot_general(
                g, weight[pl.ds(at, WIDTH), :], (((1,), (1,)), ((), ())), preferred_element_type=F32
            )
            out[j] = part.astype(BF16)


def core_sum(mine, other, out):
    for j in range(RING):
        out[j, :ROWS] = (mine[j, :ROWS].astype(F32) + other[j, :ROWS].astype(F32)).astype(BF16)
    if out.shape[1] > ROWS:
        stats = split_stats(joined_stats(mine[0, ROWS:]) + joined_stats(other[0, ROWS:]))
        for j in range(RING):
            out[j, ROWS:] = stats


def ring_sum(pieces, out):
    total = pieces[0, :ROWS].astype(F32)
    for j in range(1, pieces.shape[0]):
        total = total + pieces[j, :ROWS].astype(F32)
    out[:ROWS] = total.astype(BF16)
    if out.shape[0] > ROWS:
        stats = joined_stats(pieces[0, ROWS:])
        for j in range(1, pieces.shape[0]):
            stats = stats + joined_stats(pieces[j, ROWS:])
        out[ROWS:] = split_stats(stats)


def forward_share(own, other, out):
    total = joined_stats(own[ROWS:]) + joined_stats(other[ROWS:])
    factor = lax.rsqrt(total[0:1] / D + EPSILON)
    value = own[:ROWS].astype(F32) + other[:ROWS].astype(F32)
    out[...] = jnp.broadcast_to((down(factor) * value).astype(BF16)[None], out.shape)


def backward_share(own, other, out):
    value = (own[...].astype(F32) + other[...].astype(F32)).astype(BF16)
    out[...] = jnp.broadcast_to(value[None], out.shape)


def half(weight, out):
    out[...] = weight[...]


def forward_product(blocks, own_weight, other_weight, mine, others):
    for weight, out in ((other_weight, others), (own_weight, mine)):
        total = jnp.zeros((ROWS, WIDTH), F32)
        for j in range(RING):
            rows = weight[j * WIDTH : (j + 1) * WIDTH, :]
            total = total + jnp.dot(blocks[j], rows, preferred_element_type=F32)
        out[...] = total


def backward_product(blocks, own_weight, other_weight, mine, others):
    for weight, out in ((other_weight, others), (own_weight, mine)):
        total = jnp.zeros((ROWS, WIDTH), F32)
        for j in range(RING):
            columns = weight[:, j * WIDTH : (j + 1) * WIDTH]
            total = total + lax.dot_general(
                blocks[j], columns, (((1,), (1,)), ((), ())), preferred_element_type=F32
            )
        out[...] = total


def forward_end(x, mine, other, out):
    out[...] = (x[...].astype(F32) + (mine[...] + other[...])).astype(BF16)


def backward_middle(tick, mine, other, saved, gain, scaled_grad, dots):
    value = mine[...] + other[...]
    scaled_grad[...] = value
    terms = [saved[tick].astype(F32) * gain[...] * value]
    if tick == 0:
        for k in range(2):
            kept = saved[k].astype(F32)
            terms.append(kept * kept)
    rows = [across(jnp.sum(term, axis=1, keepdims=True)) for term in terms]
    rows.append(jnp.zeros((DOT_ROWS - len(rows), ROWS), F32))
    dots[...] = jnp.broadcast_to(jnp.concatenate(rows, axis=0)[None], dots.shape)


def backward_end(tick, g, scaled_grad, saved, gain, dots, *refs):
    before, (out, gain_out, *left) = refs[: 2 if tick else 0], refs[2 if tick else 0 :]
    total = dots[0, :8]
    for j in range(1, dots.shape[0]):
        total = total + dots[j, :8]
    if tick == 0:
        squares = total[1:2]
        left[0][...] = jnp.broadcast_to(total[2:3], left[0].shape)
    else:
        squares = before[0][0:1]
    factor = down(lax.rsqrt(squares / D + EPSILON))
    kept = saved[tick].astype(F32)
    sums = jnp.sum(scaled_grad[...] * kept * factor, axis=0, keepdims=True)
    gain_out[...] = sums + before[1][...] if tick else sums
    value = g[...].astype(F32) + factor * gain[...] * scaled_grad[...]
    out[...] = (value - kept * (factor * factor * factor) * down(total[0:1]) / D).astype(BF16)


def over(value, pairs):
    return lax.ppermute(value, "shard", pairs)


def shards(
    value_weight,
    output_weight,
    norm_gain,
    arriving,
    fresh_inputs,
    returning,
    cotangents,
    saved_inputs,
    forward_base,
    backward_base,
    sample_ids,
    forward_exponents,
    backward_exponents,
):
    segment = lax.axis_index("segment")
    segments = lax.axis_size("segment")
    position = lax.axis_index("shard")
    core = position % 2
    meta = jnp.stack([segment, position // 4, position // 2 % 2, core]).astype(jnp.int32)
    value_local, output_local = value_weight[0], output_weight[0]
    saved = saved_inputs[0]
    low = shape_of(ROWS, WIDTH)
    wide = shape_of(ROWS, WIDTH, dtype=F32)
    tall = shape_of(ROWS + STATS, WIDTH)
    eight = shape_of(RING, ROWS, WIDTH)
    eight_tall = shape_of(RING, ROWS + STATS, WIDTH)
    row = shape_of(1, WIDTH, dtype=F32)
    own_half = {1: ((HALF, WIDTH), lambda i, meta: (meta[3], 0))}
    own_columns = {1: ((WIDTH, HALF), lambda i, meta: (0, meta[3]))}

    def base_blocks(first, micro):
        return {
            first + sample: (
                (1, SEQ, WIDTH),
                lambda i, ids, meta, exps, sample=sample: (ids[micro(meta), sample], 0, 0),
            )
            for sample in range(2)
        }

    def forward_begin(tick, messages, *after):
        count = len(messages)
        x, keep, send = call(
            functools.partial(forward_start, tick, count),
            "forward_start",
            [low, eight_tall, eight_tall],
            prefetch=(sample_ids, meta, forward_exponents[0]),
            operands=(*messages, forward_base[0], forward_base[0], norm_gain, value_local),
            blocks=base_blocks(count, lambda meta: tick - meta[0] + segments - 1),
            after=after,
        )
        operands = (keep, over(send, core_pairs()))
        return x, *call(core_sum, "forward_core_sum", [eight_tall], operands=operands)

    def backward_begin(tick, messages, *after):
        count = len(messages)
        g, keep, send = call(
            functools.partial(backward_start, tick, count, segments - 1),
            "backward_start",
            [low, eight, eight],
            prefetch=(sample_ids, meta, backward_exponents[0]),
            operands=(*messages, backward_base[0], backward_base[0], output_local),
            blocks=base_blocks(count, lambda meta: tick + meta[0]),
            after=after,
        )
        operands = (keep, over(send, core_pairs()))
        return g, *call(core_sum, "backward_core_sum", [eight], operands=operands)

    def forward_turn(pieces, *after):
        (own,) = call(ring_sum, "forward_ring_sum", [tall], operands=(pieces,), after=after)
        return own, *call(forward_share, "forward_share", [eight], operands=(own, over(own, z_pairs())))

    def backward_turn(pieces, *after):
        (own,) = call(ring_sum, "backward_ring_sum", [low], operands=(pieces,), after=after)
        return own, *call(backward_share, "backward_share", [eight], operands=(own, over(own, z_pairs())))

    def with_meta(kernel):
        return lambda _, *refs: kernel(*refs)

    def exchanged_half(weight, block, index_map, *after):
        (own,) = call(
            with_meta(half),
            "half",
            [shape_of(*block)],
            prefetch=(meta,),
            operands=(weight,),
            blocks={0: (block, index_map)},
            after=after,
        )
        return over(own, core_pairs())

    def forward_finish(x, gathered, *after):
        mine, others = call(
            with_meta(forward_product),
            "forward_product",
            [wide, wide],
            prefetch=(meta,),
            operands=(gathered, output_local, output_other),
            blocks=own_half,
            after=after,
        )
        operands = (x, mine, over(others, core_pairs()))
        return call(forward_end, "forward_end", [low], operands=operands)[0]

    def backward_dots(tick, gathered, *after):
        mine, others = call(
            with_meta(backward_product),
            "backward_product",
            [wide, wide],
            prefetch=(meta,),
            operands=(gathered, value_local, value_other),
            blocks=own_columns,
            after=after,
        )
        return call(
            functools.partial(backward_middle, tick),
            "backward_middle",
            [wide, shape_of(4 * RING, DOT_ROWS, ROWS, dtype=F32)],
            operands=(mine, over(others, core_pairs()), saved, norm_gain),
        )

    def backward_finish(tick, g, scaled_grad, dots, left, *after):
        return call(
            functools.partial(backward_end, tick),
            "backward_end",
            [low, row] + ([shape_of(8, ROWS, dtype=F32)] if tick == 0 else []),
            operands=(g, scaled_grad, saved, norm_gain, dots, *left),
            after=after,
        )

    x, pieces = forward_begin(0, [arriving[0]])
    gated = gate(pieces)
    landed = swapped(gated, rings())

    g, back_pieces = backward_begin(0, [returning[0]], gated)
    gated = gate(back_pieces, landed)
    back_landed = swapped(gated, rings())

    own, copies = forward_turn(landed, gated)
    output_other = exchanged_half(output_local, (HALF, WIDTH), lambda i, meta: (1 - meta[3], 0), own)
    gated = gate(copies, back_landed, output_other)
    gathered = swapped(gated, rings())

    own, copies = backward_turn(back_landed, gated)
    value_other = exchanged_half(value_local, (WIDTH, HALF), lambda i, meta: (0, 1 - meta[3]), own)
    gated = gate(copies, gathered, value_other)
    back_gathered = swapped(gated, rings())

    segment_out = forward_finish(x, gathered, gated)
    x, pieces = forward_begin(1, [shifted(segment_out, "segment", 1), fresh_inputs])
    scaled_grad, dots = backward_dots(0, back_gathered)
    all_dots = swapped(dots)

    gated = gate(pieces, all_dots)
    landed = swapped(gated, rings())

    input_grad, gain_total, squares = backward_finish(0, g, scaled_grad, all_dots, (), gated)
    g, back_pieces = backward_begin(1, [shifted(input_grad, "segment", -1), cotangents])
    gated = gate(back_pieces, landed)
    back_landed = swapped(gated, rings())

    _, copies = forward_turn(landed, gated)
    gated = gate(copies, back_landed)
    gathered = swapped(gated, rings())

    _, copies = backward_turn(back_landed, gated)
    gated = gate(copies, gathered)
    back_gathered = swapped(gated, rings())

    segment_out = forward_finish(x, gathered, gated)
    scaled_grad, dots = backward_dots(1, back_gathered, segment_out)
    all_dots = swapped(dots)
    input_grad, gain_total = backward_finish(1, g, scaled_grad, all_dots, (squares, gain_total))
    return (segment_out[None], input_grad[None], gain_total)


def solution(mesh):
    return jax.shard_map(
        shards,
        mesh=mesh,
        in_specs=(
            P("segment", "shard", None),
            P("segment", None, "shard"),
            P("segment", "shard"),
            P("segment", None, "shard"),
            P(None, None, "shard"),
            P("segment", None, "shard"),
            P(None, None, "shard"),
            P("segment", None, None, "shard"),
            P("segment", None, None, "shard"),
            P("segment", None, None, "shard"),
            P(),
            P("segment", None, "shard"),
            P("segment", None, "shard"),
        ),
        out_specs=(P("segment", None, "shard"), P("segment", None, "shard"), P("segment", "shard")),
        check_vma=False,
    )
```

```python
import functools

import jax
import jax.numpy as jnp
from jax import lax
from jax.experimental import pallas as pl
from jax.experimental.pallas import tpu as pltpu
from jax.sharding import PartitionSpec as P

D = 8192
BLOCK = 128
ROWS = 128
WIDTH = 256
SEQ = 64
STATS = 16
RING = 8
HALF = RING * WIDTH
EPSILON = 1e-05
F32 = jnp.float32
BF16 = jnp.bfloat16
VMEM_LIMIT = 20 * 1024 * 1024
EXTRA = 8


def core_pairs():
    return [(index, index ^ 1) for index in range(4 * RING)]


def z_pairs():
    return [(index, index ^ 2) for index in range(4 * RING)]


def rings():
    return [[4 * y + rest for y in range(RING)] for rest in range(4)]


def planes():
    return [[2 * chip + core for chip in range(2 * RING)] for core in range(2)]


def swapped(value, groups):
    return lax.all_to_all(value, "shard", 0, 0, axis_index_groups=groups, tiled=True)


def gate(value, *after):
    return lax.optimization_barrier((value, *after))[0]


def shifted(value, axis, steps):
    count = lax.axis_size(axis)
    leading, last = (max(0, -steps), min(count, count - steps))
    return lax.ppermute(value, axis, [(source, source + steps) for source in range(leading, last)])


def call(kernel, name, outs, *, prefetch=(), blocks=None, operands=(), after=(), scratch=()):
    blocks = blocks or {}
    first, last = len(prefetch) + len(operands), len(prefetch) + len(operands) + len(after)

    def body(*refs):
        kernel(*refs[:first], *refs[last:])

    def spec(position, operand):
        if position in blocks:
            if blocks[position] is None:
                return pl.BlockSpec(memory_space=pl.ANY)
            shape, index_map = blocks[position]
            return pl.BlockSpec(shape, index_map)
        rank = len(operand.shape)
        return pl.BlockSpec(operand.shape, lambda *_: (0,) * rank)

    in_specs = [spec(position, operand) for position, operand in enumerate(operands)]
    return pl.pallas_call(
        body,
        out_shape=outs,
        grid_spec=pltpu.PrefetchScalarGridSpec(
            num_scalar_prefetch=len(prefetch),
            grid=(1,),
            in_specs=in_specs + [pl.BlockSpec(memory_space=pl.ANY)] * len(after),
            out_specs=[pl.BlockSpec(out.shape, lambda *_, rank=len(out.shape): (0,) * rank) for out in outs],
            scratch_shapes=scratch,
        ),
        compiler_params=pltpu.CompilerParams(vmem_limit_bytes=VMEM_LIMIT),
        cost_estimate=pl.CostEstimate(flops=0, bytes_accessed=0, transcendentals=0),
        name=name,
    )(*prefetch, *operands, *after)


def shape_of(*dims, dtype=BF16):
    return jax.ShapeDtypeStruct(dims, dtype)


def across(column):
    return jnp.broadcast_to(column, (ROWS, ROWS)).T[0:1]


def down(row):
    square = jnp.broadcast_to(row, (ROWS, ROWS)).T
    return jnp.concatenate([square, square], axis=1)


def split_stats(total):
    high = total.astype(BF16).astype(F32)
    return jnp.concatenate([high, total - high], axis=1).astype(BF16)


def joined_stats(coded):
    value = coded.astype(F32)
    return value[:, :ROWS] + value[:, ROWS:]


def power_row(low, high, sign):
    lane = lax.broadcasted_iota(jnp.int32, (1, WIDTH), 1)
    exponent = sign * jnp.where(lane < BLOCK, low, high)
    magnitude = jnp.abs(exponent)
    grown = jnp.ones((1, WIDTH), F32)
    shrunk = jnp.ones((1, WIDTH), F32)
    for bit in range(4):
        bit_set = (magnitude >> bit) & 1 == 1
        grown = jnp.where(bit_set, grown * 2.0 ** (2**bit), grown)
        shrunk = jnp.where(bit_set, shrunk * 0.5 ** (2**bit), shrunk)
    return jnp.where(exponent < 0, shrunk, grown)


def decoded(message, first_ref, second_ref, exponents, tick):
    low, high = exponents[tick, 0], exponents[tick, 1]
    scale = power_row(low, high, 1)
    inverse = power_row(low, high, -1)
    base = jnp.concatenate([first_ref[0], second_ref[0]], axis=0).astype(F32)
    delta = jnp.clip((message.astype(F32) - base) * inverse, -127.0, 127.0).astype(BF16)
    return (base + delta.astype(F32) * scale).astype(BF16)


def chosen(meta, edge, refs):
    if len(refs) == 1:
        return refs[0][...]
    return jnp.where(meta[0] == edge, refs[1][0].astype(F32), refs[0][...].astype(F32))


def forward_start(tick, messages, ids, meta, exponents, *refs):
    given, refs = refs[:messages], refs[messages:]
    first, second, gain, weight, x_out, keep, send = refs
    x = decoded(chosen(meta, 0, given), first, second, exponents, tick)
    x_out[...] = x
    x = x.astype(F32)
    scaled = (x * gain[...]).astype(BF16)
    total = across(jnp.sum(x * x, axis=1, keepdims=True))
    stats = split_stats(jnp.broadcast_to(total, (STATS, ROWS)))
    core = meta[3]
    for out, half in ((send, 1 - core), (keep, core)):
        for j in range(RING):
            at = pl.multiple_of((half * RING + j) * WIDTH, WIDTH)
            part = jnp.dot(scaled, weight[:, pl.ds(at, WIDTH)], preferred_element_type=F32)
            out[j, :ROWS] = part.astype(BF16)
            out[j, ROWS:] = stats


def backward_start(tick, messages, last, ids, meta, exponents, *refs):
    given, refs = refs[:messages], refs[messages:]
    if tick == 0:
        first, second, weight, saved, gain, g_out, keep, send, weighted, squares = refs
        rows = [jnp.zeros((1, ROWS), F32)]
        for k in range(2):
            kept = saved[k].astype(F32)
            weighted[k] = kept * gain[...]
            rows.append(across(jnp.sum(kept * kept, axis=1, keepdims=True)))
        squares[...] = jnp.concatenate(rows + [jnp.zeros((EXTRA - 3, ROWS), F32)], axis=0)
    else:
        first, second, weight, g_out, keep, send = refs
    g = decoded(chosen(meta, last, given), first, second, exponents, tick)
    g_out[...] = g
    core = meta[3]
    for out, half in ((send, 1 - core), (keep, core)):
        for j in range(RING):
            at = pl.multiple_of((half * RING + j) * WIDTH, WIDTH)
            part = lax.dot_general(
                g, weight[pl.ds(at, WIDTH), :], (((1,), (1,)), ((), ())), preferred_element_type=F32
            )
            out[j] = part.astype(BF16)


def core_sum(mine, other, out):
    for j in range(RING):
        out[j, :ROWS] = (mine[j, :ROWS].astype(F32) + other[j, :ROWS].astype(F32)).astype(BF16)
    if out.shape[1] > ROWS:
        stats = split_stats(joined_stats(mine[0, ROWS:]) + joined_stats(other[0, ROWS:]))
        for j in range(RING):
            out[j, ROWS:] = stats


def ring_sum(pieces, out):
    total = pieces[0, :ROWS].astype(F32)
    for j in range(1, pieces.shape[0]):
        total = total + pieces[j, :ROWS].astype(F32)
    out[:ROWS] = total.astype(BF16)
    if out.shape[0] > ROWS:
        stats = joined_stats(pieces[0, ROWS:])
        for j in range(1, pieces.shape[0]):
            stats = stats + joined_stats(pieces[j, ROWS:])
        out[ROWS:] = split_stats(stats)


def forward_share(own, other, *refs):
    total = joined_stats(own[ROWS:]) + joined_stats(other[ROWS:])
    factor = lax.rsqrt(total[0:1] / D + EPSILON)
    value = own[:ROWS].astype(F32) + other[:ROWS].astype(F32)
    value = (down(factor) * value).astype(BF16)
    out, *half = refs[len(refs) // 2 :]
    out[...] = jnp.broadcast_to(value[None], out.shape)
    if half:
        half[0][...] = refs[0][...]


def backward_share(own, other, *refs):
    value = (own[...].astype(F32) + other[...].astype(F32)).astype(BF16)
    out, *half = refs[len(refs) // 2 :]
    out[...] = jnp.broadcast_to(value[None], out.shape)
    if half:
        half[0][...] = refs[0][...]


def forward_product(meta, blocks, weight, other_weight, mine, others, own_weight, arrived):
    at = pl.multiple_of(meta[3] * HALF, HALF)
    copy = pltpu.make_async_copy(weight.at[pl.ds(at, HALF), :], own_weight, arrived)
    copy.start()
    for half, out in ((other_weight, others), (own_weight, mine)):
        if half is own_weight:
            copy.wait()
        total = jnp.zeros((ROWS, WIDTH), F32)
        for j in range(RING):
            rows = half[j * WIDTH : (j + 1) * WIDTH, :]
            total = total + jnp.dot(blocks[j], rows, preferred_element_type=F32)
        out[...] = total


def backward_product(meta, blocks, weight, other_weight, weighted, other_weighted, squares, mine, others, own_weight, arrived):
    at = pl.multiple_of(meta[3] * HALF, HALF)
    copy = pltpu.make_async_copy(weight.at[:, pl.ds(at, HALF)], own_weight, arrived)
    copy.start()
    dots = jnp.zeros((ROWS, 1), F32)
    for half, out, factors in ((other_weight, others, other_weighted), (own_weight, mine, weighted)):
        if half is own_weight:
            copy.wait()
        total = jnp.zeros((ROWS, WIDTH), F32)
        for j in range(RING):
            columns = half[:, j * WIDTH : (j + 1) * WIDTH]
            total = total + lax.dot_general(
                blocks[j], columns, (((1,), (1,)), ((), ())), preferred_element_type=F32
            )
        out[:ROWS] = total
        dots = dots + jnp.sum(total * factors[0], axis=1, keepdims=True)
    rows = jnp.concatenate([across(dots), squares[1:]], axis=0)
    rows = jnp.concatenate([rows, jnp.zeros_like(rows)], axis=1)
    mine[ROWS:] = rows
    others[ROWS:] = rows


def forward_end(x, mine, other, out):
    out[...] = (x[...].astype(F32) + (mine[...] + other[...])).astype(BF16)


def backward_middle(mine, other, scaled_grad, dots):
    scaled_grad[...] = mine[:ROWS] + other[:ROWS]
    rows = mine[ROWS:, :ROWS] + other[ROWS:, :ROWS]
    dots[...] = jnp.broadcast_to(rows[None], dots.shape)


def backward_end(tick, g, scaled_grad, saved, gain, dots, *refs):
    before, (out, gain_out, *left) = refs[: 2 if tick else 0], refs[2 if tick else 0 :]
    total = dots[0]
    for j in range(1, dots.shape[0]):
        total = total + dots[j]
    if tick == 0:
        squares = total[1:2]
        left[0][...] = jnp.broadcast_to(total[2:3], left[0].shape)
    else:
        squares = before[0][0:1]
    factor = down(lax.rsqrt(squares / D + EPSILON))
    kept = saved[tick].astype(F32)
    sums = jnp.sum(scaled_grad[...] * kept * factor, axis=0, keepdims=True)
    gain_out[...] = sums + before[1][...] if tick else sums
    value = g[...].astype(F32) + factor * gain[...] * scaled_grad[...]
    out[...] = (value - kept * (factor * factor * factor) * down(total[0:1]) / D).astype(BF16)


def over(value, pairs):
    return lax.ppermute(value, "shard", pairs)


def shards(
    value_weight,
    output_weight,
    norm_gain,
    arriving,
    fresh_inputs,
    returning,
    cotangents,
    saved_inputs,
    forward_base,
    backward_base,
    sample_ids,
    forward_exponents,
    backward_exponents,
):
    segment = lax.axis_index("segment")
    segments = lax.axis_size("segment")
    position = lax.axis_index("shard")
    core = position % 2
    meta = jnp.stack([segment, position // 4, position // 2 % 2, core]).astype(jnp.int32)
    value_local, output_local = value_weight[0], output_weight[0]
    saved = saved_inputs[0]
    low = shape_of(ROWS, WIDTH)
    wide = shape_of(ROWS, WIDTH, dtype=F32)
    tall = shape_of(ROWS + STATS, WIDTH)
    eight = shape_of(RING, ROWS, WIDTH)
    eight_tall = shape_of(RING, ROWS + STATS, WIDTH)
    row = shape_of(1, WIDTH, dtype=F32)
    product = shape_of(ROWS + EXTRA, WIDTH, dtype=F32)
    fetched = pltpu.SemaphoreType.DMA

    def base_blocks(first, micro):
        return {
            first + sample: (
                (1, SEQ, WIDTH),
                lambda i, ids, meta, exps, sample=sample: (ids[micro(meta), sample], 0, 0),
            )
            for sample in range(2)
        }

    def forward_begin(tick, messages, *after):
        count = len(messages)
        x, keep, send = call(
            functools.partial(forward_start, tick, count),
            "forward_start",
            [low, eight_tall, eight_tall],
            prefetch=(sample_ids, meta, forward_exponents[0]),
            operands=(*messages, forward_base[0], forward_base[0], norm_gain, value_local),
            blocks=base_blocks(count, lambda meta: tick - meta[0] + segments - 1),
            after=after,
        )
        operands = (keep, over(send, core_pairs()))
        return x, *call(core_sum, "forward_core_sum", [eight_tall], operands=operands)

    def backward_begin(tick, messages, *after):
        count = len(messages)
        outs, extra = [low, eight, eight], ()
        if tick == 0:
            outs += [shape_of(2, ROWS, WIDTH, dtype=F32), shape_of(EXTRA, ROWS, dtype=F32)]
            extra = (saved, norm_gain)
        g, keep, send, *rest = call(
            functools.partial(backward_start, tick, count, segments - 1),
            "backward_start",
            outs,
            prefetch=(sample_ids, meta, backward_exponents[0]),
            operands=(*messages, backward_base[0], backward_base[0], output_local, *extra),
            blocks=base_blocks(count, lambda meta: tick + meta[0]),
            after=after,
        )
        operands = (keep, over(send, core_pairs()))
        return g, *call(core_sum, "backward_core_sum", [eight], operands=operands), *rest

    def turn(kernel, name, block, pieces, half, *after):
        (own,) = call(ring_sum, name + "_ring_sum", [block], operands=(pieces,), after=after)
        operands, outs, blocks = (own, over(own, z_pairs())), [eight], {}
        if half:
            weight, shape, index_map = half
            operands, outs, blocks = (*operands, weight), [eight, shape_of(*shape)], {2: (shape, index_map)}
        return call(with_meta(kernel), name + "_share", outs, prefetch=(meta,), operands=operands, blocks=blocks)

    def with_meta(kernel):
        return lambda _, *refs: kernel(*refs)

    def forward_finish(x, gathered, *after):
        mine, others = call(
            forward_product,
            "forward_product",
            [wide, wide],
            prefetch=(meta,),
            operands=(gathered, output_local, output_other),
            blocks={1: None},
            after=after,
            scratch=(pltpu.VMEM((HALF, WIDTH), BF16), fetched),
        )
        operands = (x, mine, over(others, core_pairs()))
        return call(forward_end, "forward_end", [low], operands=operands)[0]

    def backward_dots(tick, gathered, *after):
        one = ((1, ROWS, WIDTH), lambda i, meta: (tick, 0, 0))
        mine, others = call(
            backward_product,
            "backward_product",
            [product, product],
            prefetch=(meta,),
            operands=(gathered, value_local, value_other, weighted, other_weighted, squares),
            blocks={1: None, 3: one, 4: one},
            after=after,
            scratch=(pltpu.VMEM((WIDTH, HALF), BF16), fetched),
        )
        operands = (mine, over(others, core_pairs()))
        outs = [wide, shape_of(2 * RING, EXTRA, ROWS, dtype=F32)]
        return call(backward_middle, "backward_middle", outs, operands=operands)

    def backward_finish(tick, g, scaled_grad, dots, left, *after):
        return call(
            functools.partial(backward_end, tick),
            "backward_end",
            [low, row] + ([shape_of(8, ROWS, dtype=F32)] if tick == 0 else []),
            operands=(g, scaled_grad, saved, norm_gain, dots, *left),
            after=after,
        )

    x, pieces = forward_begin(0, [arriving[0]])
    gated = gate(pieces)
    landed = swapped(gated, rings())

    g, back_pieces, weighted, squares = backward_begin(0, [returning[0]], gated)
    other_weighted = over(weighted, core_pairs())
    gated = gate(back_pieces, landed)
    back_landed = swapped(gated, rings())

    half = (output_local, (HALF, WIDTH), lambda i, meta: (1 - meta[3], 0))
    copies, half = turn(forward_share, "forward", tall, landed, half, gated)
    output_other = over(half, core_pairs())
    gated = gate(copies, back_landed)
    gathered = swapped(gated, rings())

    half = (value_local, (WIDTH, HALF), lambda i, meta: (0, 1 - meta[3]))
    copies, half = turn(backward_share, "backward", low, back_landed, half, gated)
    value_other = over(half, core_pairs())
    gated = gate(copies, gathered)
    back_gathered = swapped(gated, rings())

    segment_out = forward_finish(x, gathered, gated)
    x, pieces = forward_begin(1, [shifted(segment_out, "segment", 1), fresh_inputs])
    scaled_grad, dots = backward_dots(0, back_gathered)
    all_dots = swapped(dots, planes())

    gated = gate(pieces, all_dots)
    landed = swapped(gated, rings())

    input_grad, gain_total, saved_squares = backward_finish(0, g, scaled_grad, all_dots, (), gated)
    g, back_pieces = backward_begin(1, [shifted(input_grad, "segment", -1), cotangents])
    gated = gate(back_pieces, landed)
    back_landed = swapped(gated, rings())

    (copies,) = turn(forward_share, "forward", tall, landed, None, gated)
    gated = gate(copies, back_landed)
    gathered = swapped(gated, rings())

    (copies,) = turn(backward_share, "backward", low, back_landed, None, gated)
    gated = gate(copies, gathered)
    back_gathered = swapped(gated, rings())

    segment_out = forward_finish(x, gathered, gated)
    scaled_grad, dots = backward_dots(1, back_gathered, segment_out)
    all_dots = swapped(dots, planes())
    input_grad, gain_total = backward_finish(1, g, scaled_grad, all_dots, (saved_squares, gain_total))
    return (segment_out[None], input_grad[None], gain_total)


def solution(mesh):
    return jax.shard_map(
        shards,
        mesh=mesh,
        in_specs=(
            P("segment", "shard", None),
            P("segment", None, "shard"),
            P("segment", "shard"),
            P("segment", None, "shard"),
            P(None, None, "shard"),
            P("segment", None, "shard"),
            P(None, None, "shard"),
            P("segment", None, None, "shard"),
            P("segment", None, None, "shard"),
            P("segment", None, None, "shard"),
            P(),
            P("segment", None, "shard"),
            P("segment", None, "shard"),
        ),
        out_specs=(P("segment", None, "shard"), P("segment", None, "shard"), P("segment", "shard")),
        check_vma=False,
    )
```

```python
import functools

import jax
import jax.numpy as jnp
from jax import lax
from jax.experimental import pallas as pl
from jax.experimental.pallas import tpu as pltpu
from jax.sharding import PartitionSpec as P

D = 8192
BLOCK = 128
ROWS = 128
WIDTH = 256
SEQ = 64
STATS = 16
RING = 8
HALF = RING * WIDTH
EPSILON = 1e-05
F32 = jnp.float32
BF16 = jnp.bfloat16
VMEM_LIMIT = 20 * 1024 * 1024
DOT_ROWS = 8


def core_pairs():
    return [(index, index ^ 1) for index in range(4 * RING)]


def z_pairs():
    return [(index, index ^ 2) for index in range(4 * RING)]


def rings():
    return [[4 * y + rest for y in range(RING)] for rest in range(4)]


def swapped(value, groups=None):
    return lax.all_to_all(value, "shard", 0, 0, axis_index_groups=groups, tiled=True)


def gate(value, *after):
    return lax.optimization_barrier((value, *after))[0]


def shifted(value, axis, steps):
    count = lax.axis_size(axis)
    leading, last = (max(0, -steps), min(count, count - steps))
    return lax.ppermute(value, axis, [(source, source + steps) for source in range(leading, last)])


def call(kernel, name, outs, *, prefetch=(), blocks=None, operands=(), after=()):
    blocks = blocks or {}
    first, last = len(prefetch) + len(operands), len(prefetch) + len(operands) + len(after)

    def body(*refs):
        kernel(*refs[:first], *refs[last:])

    def spec(position, operand):
        if position in blocks:
            shape, index_map = blocks[position]
            return pl.BlockSpec(shape, index_map)
        rank = len(operand.shape)
        return pl.BlockSpec(operand.shape, lambda *_: (0,) * rank)

    in_specs = [spec(position, operand) for position, operand in enumerate(operands)]
    return pl.pallas_call(
        body,
        out_shape=outs,
        grid_spec=pltpu.PrefetchScalarGridSpec(
            num_scalar_prefetch=len(prefetch),
            grid=(1,),
            in_specs=in_specs + [pl.BlockSpec(memory_space=pl.ANY)] * len(after),
            out_specs=[pl.BlockSpec(out.shape, lambda *_, rank=len(out.shape): (0,) * rank) for out in outs],
        ),
        compiler_params=pltpu.CompilerParams(vmem_limit_bytes=VMEM_LIMIT),
        cost_estimate=pl.CostEstimate(flops=0, bytes_accessed=0, transcendentals=0),
        name=name,
    )(*prefetch, *operands, *after)


def shape_of(*dims, dtype=BF16):
    return jax.ShapeDtypeStruct(dims, dtype)


def across(column):
    return jnp.broadcast_to(column, (ROWS, ROWS)).T[0:1]


def down(row):
    square = jnp.broadcast_to(row, (ROWS, ROWS)).T
    return jnp.concatenate([square, square], axis=1)


def split_stats(total):
    high = total.astype(BF16).astype(F32)
    return jnp.concatenate([high, total - high], axis=1).astype(BF16)


def joined_stats(coded):
    value = coded.astype(F32)
    return value[:, :ROWS] + value[:, ROWS:]


def power_row(low, high, sign):
    lane = lax.broadcasted_iota(jnp.int32, (1, WIDTH), 1)
    exponent = sign * jnp.where(lane < BLOCK, low, high)
    magnitude = jnp.abs(exponent)
    grown = jnp.ones((1, WIDTH), F32)
    shrunk = jnp.ones((1, WIDTH), F32)
    for bit in range(4):
        bit_set = (magnitude >> bit) & 1 == 1
        grown = jnp.where(bit_set, grown * 2.0 ** (2**bit), grown)
        shrunk = jnp.where(bit_set, shrunk * 0.5 ** (2**bit), shrunk)
    return jnp.where(exponent < 0, shrunk, grown)


def decoded(message, first_ref, second_ref, exponents, tick):
    low, high = exponents[tick, 0], exponents[tick, 1]
    scale = power_row(low, high, 1)
    inverse = power_row(low, high, -1)
    base = jnp.concatenate([first_ref[0], second_ref[0]], axis=0).astype(F32)
    delta = jnp.clip((message.astype(F32) - base) * inverse, -127.0, 127.0).astype(BF16)
    return (base + delta.astype(F32) * scale).astype(BF16)


def chosen(meta, edge, refs):
    if len(refs) == 1:
        return refs[0][...]
    return jnp.where(meta[0] == edge, refs[1][0].astype(F32), refs[0][...].astype(F32))


def forward_start(tick, messages, ids, meta, exponents, *refs):
    given, refs = refs[:messages], refs[messages:]
    first, second, gain, weight, x_out, keep, send = refs
    x = decoded(chosen(meta, 0, given), first, second, exponents, tick)
    x_out[...] = x
    x = x.astype(F32)
    scaled = (x * gain[...]).astype(BF16)
    total = across(jnp.sum(x * x, axis=1, keepdims=True))
    stats = split_stats(jnp.broadcast_to(total, (STATS, ROWS)))
    core = meta[3]
    for out, half in ((send, 1 - core), (keep, core)):
        for j in range(RING):
            at = pl.multiple_of((half * RING + j) * WIDTH, WIDTH)
            part = jnp.dot(scaled, weight[:, pl.ds(at, WIDTH)], preferred_element_type=F32)
            out[j, :ROWS] = part.astype(BF16)
            out[j, ROWS:] = stats


def backward_start(tick, messages, last, ids, meta, exponents, *refs):
    given, (first, second, weight, g_out, keep, send) = refs[:messages], refs[messages:]
    g = decoded(chosen(meta, last, given), first, second, exponents, tick)
    g_out[...] = g
    core = meta[3]
    for out, half in ((send, 1 - core), (keep, core)):
        for j in range(RING):
            at = pl.multiple_of((half * RING + j) * WIDTH, WIDTH)
            part = lax.dot_general(
                g, weight[pl.ds(at, WIDTH), :], (((1,), (1,)), ((), ())), preferred_element_type=F32
            )
            out[j] = part.astype(BF16)


def core_sum(mine, other, out):
    for j in range(RING):
        out[j, :ROWS] = (mine[j, :ROWS].astype(F32) + other[j, :ROWS].astype(F32)).astype(BF16)
    if out.shape[1] > ROWS:
        stats = split_stats(joined_stats(mine[0, ROWS:]) + joined_stats(other[0, ROWS:]))
        for j in range(RING):
            out[j, ROWS:] = stats


def ring_sum(pieces, out):
    total = pieces[0, :ROWS].astype(F32)
    for j in range(1, pieces.shape[0]):
        total = total + pieces[j, :ROWS].astype(F32)
    out[:ROWS] = total.astype(BF16)
    if out.shape[0] > ROWS:
        stats = joined_stats(pieces[0, ROWS:])
        for j in range(1, pieces.shape[0]):
            stats = stats + joined_stats(pieces[j, ROWS:])
        out[ROWS:] = split_stats(stats)


def forward_share(own, other, *refs):
    total = joined_stats(own[ROWS:]) + joined_stats(other[ROWS:])
    factor = lax.rsqrt(total[0:1] / D + EPSILON)
    value = own[:ROWS].astype(F32) + other[:ROWS].astype(F32)
    value = (down(factor) * value).astype(BF16)
    out, *half = refs[len(refs) // 2 :]
    out[...] = jnp.broadcast_to(value[None], out.shape)
    if half:
        half[0][...] = refs[0][...]


def backward_share(own, other, *refs):
    value = (own[...].astype(F32) + other[...].astype(F32)).astype(BF16)
    out, *half = refs[len(refs) // 2 :]
    out[...] = jnp.broadcast_to(value[None], out.shape)
    if half:
        half[0][...] = refs[0][...]


def forward_product(blocks, own_weight, other_weight, mine, others):
    for weight, out in ((other_weight, others), (own_weight, mine)):
        total = jnp.zeros((ROWS, WIDTH), F32)
        for j in range(RING):
            rows = weight[j * WIDTH : (j + 1) * WIDTH, :]
            total = total + jnp.dot(blocks[j], rows, preferred_element_type=F32)
        out[...] = total


def backward_product(blocks, own_weight, other_weight, mine, others):
    for weight, out in ((other_weight, others), (own_weight, mine)):
        total = jnp.zeros((ROWS, WIDTH), F32)
        for j in range(RING):
            columns = weight[:, j * WIDTH : (j + 1) * WIDTH]
            total = total + lax.dot_general(
                blocks[j], columns, (((1,), (1,)), ((), ())), preferred_element_type=F32
            )
        out[...] = total


def forward_end(x, mine, other, out):
    out[...] = (x[...].astype(F32) + (mine[...] + other[...])).astype(BF16)


def backward_middle(tick, mine, other, saved, gain, scaled_grad, dots):
    value = mine[...] + other[...]
    scaled_grad[...] = value
    terms = [saved[tick].astype(F32) * gain[...] * value]
    if tick == 0:
        for k in range(2):
            kept = saved[k].astype(F32)
            terms.append(kept * kept)
    rows = [across(jnp.sum(term, axis=1, keepdims=True)) for term in terms]
    rows.append(jnp.zeros((DOT_ROWS - len(rows), ROWS), F32))
    dots[...] = jnp.broadcast_to(jnp.concatenate(rows, axis=0)[None], dots.shape)


def backward_end(tick, g, scaled_grad, saved, gain, dots, *refs):
    before, (out, gain_out, *left) = refs[: 2 if tick else 0], refs[2 if tick else 0 :]
    total = dots[0, :8]
    for j in range(1, dots.shape[0]):
        total = total + dots[j, :8]
    if tick == 0:
        squares = total[1:2]
        left[0][...] = jnp.broadcast_to(total[2:3], left[0].shape)
    else:
        squares = before[0][0:1]
    factor = down(lax.rsqrt(squares / D + EPSILON))
    kept = saved[tick].astype(F32)
    sums = jnp.sum(scaled_grad[...] * kept * factor, axis=0, keepdims=True)
    gain_out[...] = sums + before[1][...] if tick else sums
    value = g[...].astype(F32) + factor * gain[...] * scaled_grad[...]
    out[...] = (value - kept * (factor * factor * factor) * down(total[0:1]) / D).astype(BF16)


def over(value, pairs):
    return lax.ppermute(value, "shard", pairs)


def shards(
    value_weight,
    output_weight,
    norm_gain,
    arriving,
    fresh_inputs,
    returning,
    cotangents,
    saved_inputs,
    forward_base,
    backward_base,
    sample_ids,
    forward_exponents,
    backward_exponents,
):
    segment = lax.axis_index("segment")
    segments = lax.axis_size("segment")
    position = lax.axis_index("shard")
    core = position % 2
    meta = jnp.stack([segment, position // 4, position // 2 % 2, core]).astype(jnp.int32)
    value_local, output_local = value_weight[0], output_weight[0]
    saved = saved_inputs[0]
    low = shape_of(ROWS, WIDTH)
    wide = shape_of(ROWS, WIDTH, dtype=F32)
    tall = shape_of(ROWS + STATS, WIDTH)
    eight = shape_of(RING, ROWS, WIDTH)
    eight_tall = shape_of(RING, ROWS + STATS, WIDTH)
    row = shape_of(1, WIDTH, dtype=F32)
    own_half = {1: ((HALF, WIDTH), lambda i, meta: (meta[3], 0))}
    own_columns = {1: ((WIDTH, HALF), lambda i, meta: (0, meta[3]))}

    def base_blocks(first, micro):
        return {
            first + sample: (
                (1, SEQ, WIDTH),
                lambda i, ids, meta, exps, sample=sample: (ids[micro(meta), sample], 0, 0),
            )
            for sample in range(2)
        }

    def forward_begin(tick, messages, *after):
        count = len(messages)
        x, keep, send = call(
            functools.partial(forward_start, tick, count),
            "forward_start",
            [low, eight_tall, eight_tall],
            prefetch=(sample_ids, meta, forward_exponents[0]),
            operands=(*messages, forward_base[0], forward_base[0], norm_gain, value_local),
            blocks=base_blocks(count, lambda meta: tick - meta[0] + segments - 1),
            after=after,
        )
        operands = (keep, over(send, core_pairs()))
        return x, *call(core_sum, "forward_core_sum", [eight_tall], operands=operands)

    def backward_begin(tick, messages, *after):
        count = len(messages)
        g, keep, send = call(
            functools.partial(backward_start, tick, count, segments - 1),
            "backward_start",
            [low, eight, eight],
            prefetch=(sample_ids, meta, backward_exponents[0]),
            operands=(*messages, backward_base[0], backward_base[0], output_local),
            blocks=base_blocks(count, lambda meta: tick + meta[0]),
            after=after,
        )
        operands = (keep, over(send, core_pairs()))
        return g, *call(core_sum, "backward_core_sum", [eight], operands=operands)

    def turn(kernel, name, block, pieces, half, *after):
        (own,) = call(ring_sum, name + "_ring_sum", [block], operands=(pieces,), after=after)
        operands, outs, blocks = (own, over(own, z_pairs())), [eight], {}
        if half:
            weight, shape, index_map = half
            operands, outs, blocks = (*operands, weight), [eight, shape_of(*shape)], {2: (shape, index_map)}
        return call(with_meta(kernel), name + "_share", outs, prefetch=(meta,), operands=operands, blocks=blocks)

    def with_meta(kernel):
        return lambda _, *refs: kernel(*refs)

    def forward_finish(x, gathered, *after):
        mine, others = call(
            with_meta(forward_product),
            "forward_product",
            [wide, wide],
            prefetch=(meta,),
            operands=(gathered, output_local, output_other),
            blocks=own_half,
            after=after,
        )
        operands = (x, mine, over(others, core_pairs()))
        return call(forward_end, "forward_end", [low], operands=operands)[0]

    def backward_dots(tick, gathered, *after):
        mine, others = call(
            with_meta(backward_product),
            "backward_product",
            [wide, wide],
            prefetch=(meta,),
            operands=(gathered, value_local, value_other),
            blocks=own_columns,
            after=after,
        )
        return call(
            functools.partial(backward_middle, tick),
            "backward_middle",
            [wide, shape_of(4 * RING, DOT_ROWS, ROWS, dtype=F32)],
            operands=(mine, over(others, core_pairs()), saved, norm_gain),
        )

    def backward_finish(tick, g, scaled_grad, dots, left, *after):
        return call(
            functools.partial(backward_end, tick),
            "backward_end",
            [low, row] + ([shape_of(8, ROWS, dtype=F32)] if tick == 0 else []),
            operands=(g, scaled_grad, saved, norm_gain, dots, *left),
            after=after,
        )

    g, back_pieces = backward_begin(0, [returning[0]])
    gated = gate(back_pieces)
    back_landed = swapped(gated, rings())

    x, pieces = forward_begin(0, [arriving[0]], gated)
    gated = gate(pieces, back_landed)
    landed = swapped(gated, rings())

    half = (value_local, (WIDTH, HALF), lambda i, meta: (0, 1 - meta[3]))
    back_copies, half = turn(backward_share, "backward", low, back_landed, half, gated)
    value_other = over(half, core_pairs())
    gated = gate(back_copies, landed)
    back_gathered = swapped(gated, rings())

    half = (output_local, (HALF, WIDTH), lambda i, meta: (1 - meta[3], 0))
    copies, half = turn(forward_share, "forward", tall, landed, half, gated)
    output_other = over(half, core_pairs())
    scaled_grad, dots = backward_dots(0, back_gathered, copies)
    all_dots = swapped(dots)

    gated = gate(copies, all_dots)
    gathered = swapped(gated, rings())

    input_grad, gain_total, squares = backward_finish(0, g, scaled_grad, all_dots, (), gated)
    g, back_pieces = backward_begin(1, [shifted(input_grad, "segment", -1), cotangents])
    gated = gate(back_pieces, gathered)
    back_landed = swapped(gated, rings())

    segment_out = forward_finish(x, gathered, gated)
    x, pieces = forward_begin(1, [shifted(segment_out, "segment", 1), fresh_inputs])
    gated = gate(pieces, back_landed)
    landed = swapped(gated, rings())

    (back_copies,) = turn(backward_share, "backward", low, back_landed, None, gated)
    gated = gate(back_copies, landed)
    back_gathered = swapped(gated, rings())

    (copies,) = turn(forward_share, "forward", tall, landed, None, gated)
    gated = gate(copies, back_gathered)
    gathered = swapped(gated, rings())

    scaled_grad, dots = backward_dots(1, back_gathered, gated)
    gated = gate(dots, gathered)
    all_dots = swapped(gated)

    segment_out = forward_finish(x, gathered, gated)
    input_grad, gain_total = backward_finish(1, g, scaled_grad, all_dots, (squares, gain_total))
    return (segment_out[None], input_grad[None], gain_total)


def solution(mesh):
    return jax.shard_map(
        shards,
        mesh=mesh,
        in_specs=(
            P("segment", "shard", None),
            P("segment", None, "shard"),
            P("segment", "shard"),
            P("segment", None, "shard"),
            P(None, None, "shard"),
            P("segment", None, "shard"),
            P(None, None, "shard"),
            P("segment", None, None, "shard"),
            P("segment", None, None, "shard"),
            P("segment", None, None, "shard"),
            P(),
            P("segment", None, "shard"),
            P("segment", None, "shard"),
        ),
        out_specs=(P("segment", None, "shard"), P("segment", None, "shard"), P("segment", "shard")),
        check_vma=False,
    )
```

```python
import functools

import jax
import jax.numpy as jnp
from jax import lax
from jax.experimental import pallas as pl
from jax.experimental.pallas import tpu as pltpu
from jax.sharding import PartitionSpec as P

D = 8192
BLOCK = 128
ROWS = 128
WIDTH = 256
SEQ = 64
RING = 8
HALF = RING * WIDTH
EPSILON = 1e-05
F32 = jnp.float32
BF16 = jnp.bfloat16
VMEM_LIMIT = 20 * 1024 * 1024
DOT_ROWS = 8
SEGMENT_AT, CORE_AT, FORWARD_AT, BACKWARD_AT = 34, 35, 36, 40


def core_pairs():
    return [(index, index ^ 1) for index in range(4 * RING)]


def z_pairs():
    return [(index, index ^ 2) for index in range(4 * RING)]


def rings():
    return [[4 * y + rest for y in range(RING)] for rest in range(4)]


def swapped(value, groups=None):
    return lax.all_to_all(value, "shard", 0, 0, axis_index_groups=groups, tiled=True)


def gate(value, *after):
    return lax.optimization_barrier((value, *after))[0]


def shifted(value, axis, steps):
    count = lax.axis_size(axis)
    leading, last = (max(0, -steps), min(count, count - steps))
    return lax.ppermute(value, axis, [(source, source + steps) for source in range(leading, last)])


def call(kernel, name, outs, *, prefetch=(), blocks=None, operands=(), after=()):
    blocks = blocks or {}
    first, last = len(prefetch) + len(operands), len(prefetch) + len(operands) + len(after)

    def body(*refs):
        kernel(*refs[:first], *refs[last:])

    def spec(position, operand):
        if position in blocks:
            shape, index_map = blocks[position]
            return pl.BlockSpec(shape, index_map)
        rank = len(operand.shape)
        return pl.BlockSpec(operand.shape, lambda *_: (0,) * rank)

    in_specs = [spec(position, operand) for position, operand in enumerate(operands)]
    return pl.pallas_call(
        body,
        out_shape=outs,
        grid_spec=pltpu.PrefetchScalarGridSpec(
            num_scalar_prefetch=len(prefetch),
            grid=(1,),
            in_specs=in_specs + [pl.BlockSpec(memory_space=pl.ANY)] * len(after),
            out_specs=[pl.BlockSpec(out.shape, lambda *_, rank=len(out.shape): (0,) * rank) for out in outs],
        ),
        compiler_params=pltpu.CompilerParams(vmem_limit_bytes=VMEM_LIMIT),
        cost_estimate=pl.CostEstimate(flops=0, bytes_accessed=0, transcendentals=0),
        name=name,
    )(*prefetch, *operands, *after)


def shape_of(*dims, dtype=BF16):
    return jax.ShapeDtypeStruct(dims, dtype)


def across(column):
    return jnp.broadcast_to(column, (ROWS, ROWS)).T[0:1]


def down(row):
    square = jnp.broadcast_to(row, (ROWS, ROWS)).T
    return jnp.concatenate([square, square], axis=1)


def power_row(low, high, sign):
    lane = lax.broadcasted_iota(jnp.int32, (1, WIDTH), 1)
    exponent = sign * jnp.where(lane < BLOCK, low, high)
    magnitude = jnp.abs(exponent)
    grown = jnp.ones((1, WIDTH), F32)
    shrunk = jnp.ones((1, WIDTH), F32)
    for bit in range(4):
        bit_set = (magnitude >> bit) & 1 == 1
        grown = jnp.where(bit_set, grown * 2.0 ** (2**bit), grown)
        shrunk = jnp.where(bit_set, shrunk * 0.5 ** (2**bit), shrunk)
    return jnp.where(exponent < 0, shrunk, grown)


def decoded(message, first_ref, second_ref, scalars, at):
    low, high = scalars[at], scalars[at + 1]
    scale = power_row(low, high, 1)
    inverse = power_row(low, high, -1)
    base = jnp.concatenate([first_ref[0], second_ref[0]], axis=0).astype(F32)
    delta = jnp.clip((message.astype(F32) - base) * inverse, -127.0, 127.0).astype(BF16)
    return (base + delta.astype(F32) * scale).astype(BF16)


def chosen(scalars, edge, refs):
    if len(refs) == 1:
        return refs[0][...]
    return jnp.where(scalars[SEGMENT_AT] == edge, refs[1][0].astype(F32), refs[0][...].astype(F32))


def forward_start(tick, messages, scalars, *refs):
    given, (first, second, gain, weight, x_out, keep, send, squares) = refs[:messages], refs[messages:]
    x = decoded(chosen(scalars, 0, given), first, second, scalars, FORWARD_AT + 2 * tick)
    x_out[...] = x
    x = x.astype(F32)
    scaled = (x * gain[...]).astype(BF16)
    squares[...] = jnp.broadcast_to(across(jnp.sum(x * x, axis=1, keepdims=True)), squares.shape)
    core = scalars[CORE_AT]
    for out, half in ((send, 1 - core), (keep, core)):
        for j in range(RING):
            at = pl.multiple_of((half * RING + j) * WIDTH, WIDTH)
            part = jnp.dot(scaled, weight[:, pl.ds(at, WIDTH)], preferred_element_type=F32)
            out[j] = part.astype(BF16)


def backward_start(tick, messages, last, scalars, *refs):
    given, (first, second, weight, g_out, keep, send) = refs[:messages], refs[messages:]
    g = decoded(chosen(scalars, last, given), first, second, scalars, BACKWARD_AT + 2 * tick)
    g_out[...] = g
    core = scalars[CORE_AT]
    for out, half in ((send, 1 - core), (keep, core)):
        for j in range(RING):
            at = pl.multiple_of((half * RING + j) * WIDTH, WIDTH)
            part = lax.dot_general(
                g, weight[pl.ds(at, WIDTH), :], (((1,), (1,)), ((), ())), preferred_element_type=F32
            )
            out[j] = part.astype(BF16)


def core_sum(mine, other, out):
    for j in range(RING):
        out[j] = (mine[j].astype(F32) + other[j].astype(F32)).astype(BF16)


def ring_sum(pieces, out):
    total = pieces[0].astype(F32)
    for j in range(1, RING):
        total = total + pieces[j].astype(F32)
    out[...] = total.astype(BF16)


def share(own, other, *refs):
    value = (own[...].astype(F32) + other[...].astype(F32)).astype(BF16)
    out, *half = refs[len(refs) // 2 :]
    out[...] = jnp.broadcast_to(value[None], out.shape)
    if half:
        half[0][...] = refs[0][...]


def forward_product(blocks, own_weight, other_weight, mine, others):
    for weight, out in ((other_weight, others), (own_weight, mine)):
        total = jnp.zeros((ROWS, WIDTH), F32)
        for j in range(RING):
            rows = weight[j * WIDTH : (j + 1) * WIDTH, :]
            total = total + jnp.dot(blocks[j], rows, preferred_element_type=F32)
        out[...] = total


def backward_product(blocks, own_weight, other_weight, mine, others):
    for weight, out in ((other_weight, others), (own_weight, mine)):
        total = jnp.zeros((ROWS, WIDTH), F32)
        for j in range(RING):
            columns = weight[:, j * WIDTH : (j + 1) * WIDTH]
            total = total + lax.dot_general(
                blocks[j], columns, (((1,), (1,)), ((), ())), preferred_element_type=F32
            )
        out[...] = total


def row_factor(squares):
    return down(lax.rsqrt(squares / D + EPSILON))


def forward_sum(x, mine, other, squares):
    return (x[...].astype(F32) + row_factor(squares) * (mine[...] + other[...])).astype(BF16)


def forward_end(x, mine, other, totals, out):
    out[...] = forward_sum(x, mine, other, totals[3:4])


def backward_middle(tick, mine, other, saved, gain, g, squares, packed, dots):
    value = mine[...] + other[...]
    packed[:ROWS] = value
    packed[ROWS : 2 * ROWS] = g[...].astype(F32)
    packed[2 * ROWS :] = jnp.broadcast_to(gain[...], (8, WIDTH))
    terms = [saved[tick].astype(F32) * gain[...] * value]
    if tick == 0:
        for k in range(2):
            kept = saved[k].astype(F32)
            terms.append(kept * kept)
    rows = [across(jnp.sum(term, axis=1, keepdims=True)) for term in terms]
    rows += [jnp.zeros((1, ROWS), F32)] * (3 - len(rows))
    rows += [squares[:1], jnp.zeros((DOT_ROWS - 4, ROWS), F32)]
    dots[...] = jnp.broadcast_to(jnp.concatenate(rows, axis=0)[None], dots.shape)


def backward_end(tick, packed, saved, dots, *refs):
    total = dots[0]
    for j in range(1, dots.shape[0]):
        total = total + dots[j]
    if tick == 0:
        out, gain_out, totals = refs
        totals[...] = total
        squares = total[1:2]
    else:
        before, gain_before, x, mine, other, out, gain_out, segment_out = refs
        segment_out[...] = forward_sum(x, mine, other, total[3:4])
        squares = before[2:3]
    factor = row_factor(squares)
    kept = saved[tick].astype(F32)
    scaled_grad, g, gain = packed[:ROWS], packed[ROWS : 2 * ROWS], packed[2 * ROWS : 2 * ROWS + 1]
    sums = jnp.sum(scaled_grad * kept * factor, axis=0, keepdims=True)
    gain_out[...] = sums + gain_before[...] if tick else sums
    value = g + factor * gain * scaled_grad
    out[...] = (value - kept * (factor * factor * factor) * down(total[0:1]) / D).astype(BF16)


def over(value, pairs):
    return lax.ppermute(value, "shard", pairs)


def shards(
    value_weight,
    output_weight,
    norm_gain,
    arriving,
    fresh_inputs,
    returning,
    cotangents,
    saved_inputs,
    forward_base,
    backward_base,
    sample_ids,
    forward_exponents,
    backward_exponents,
):
    segment = lax.axis_index("segment")
    segments = lax.axis_size("segment")
    position = lax.axis_index("shard")
    core = position % 2
    numbers = (sample_ids, jnp.stack([segment, core]), forward_exponents, backward_exponents)
    scalars = jnp.concatenate([number.astype(jnp.int32).reshape(-1) for number in numbers])
    value_local, output_local = value_weight[0], output_weight[0]
    saved = saved_inputs[0]
    low = shape_of(ROWS, WIDTH)
    wide = shape_of(ROWS, WIDTH, dtype=F32)
    eight = shape_of(RING, ROWS, WIDTH)
    row = shape_of(1, WIDTH, dtype=F32)
    small = shape_of(DOT_ROWS, ROWS, dtype=F32)
    own_half = {1: ((HALF, WIDTH), lambda i, scalars: (scalars[CORE_AT], 0))}
    own_columns = {1: ((WIDTH, HALF), lambda i, scalars: (0, scalars[CORE_AT]))}

    def base_blocks(first, micro):
        return {
            first + sample: (
                (1, SEQ, WIDTH),
                lambda i, scalars, sample=sample: (scalars[2 * micro(scalars[SEGMENT_AT]) + sample], 0, 0),
            )
            for sample in range(2)
        }

    def run(kernel, name, outs, operands, blocks=None, after=()):
        return call(kernel, name, outs, prefetch=(scalars,), operands=operands, blocks=blocks, after=after)

    def plain(kernel):
        return lambda _, *refs: kernel(*refs)

    def forward_begin(tick, messages, *after):
        count = len(messages)
        x, keep, send, squares = run(
            functools.partial(forward_start, tick, count),
            "forward_start",
            [low, eight, eight, small],
            (*messages, forward_base[0], forward_base[0], norm_gain, value_local),
            base_blocks(count, lambda segment: tick - segment + segments - 1),
            after,
        )
        operands = (keep, over(send, core_pairs()))
        return x, squares, *call(core_sum, "forward_core_sum", [eight], operands=operands)

    def backward_begin(tick, messages, *after):
        count = len(messages)
        g, keep, send = run(
            functools.partial(backward_start, tick, count, segments - 1),
            "backward_start",
            [low, eight, eight],
            (*messages, backward_base[0], backward_base[0], output_local),
            base_blocks(count, lambda segment: tick + segment),
            after,
        )
        operands = (keep, over(send, core_pairs()))
        return g, *call(core_sum, "backward_core_sum", [eight], operands=operands)

    def turn(name, pieces, half, *after):
        (own,) = call(ring_sum, name + "_ring_sum", [low], operands=(pieces,), after=after)
        operands, outs, blocks = (own, over(own, z_pairs())), [eight], {}
        if half:
            weight, shape, index_map = half
            operands, outs, blocks = (*operands, weight), [eight, shape_of(*shape)], {2: (shape, index_map)}
        return run(plain(share), name + "_share", outs, operands, blocks)

    def forward_product_of(gathered, *after):
        operands = (gathered, output_local, output_other)
        mine, others = run(plain(forward_product), "forward_product", [wide, wide], operands, own_half, after)
        return mine, over(others, core_pairs())

    def backward_dots(tick, gathered, g, squares, *after):
        operands = (gathered, value_local, value_other)
        mine, others = run(plain(backward_product), "backward_product", [wide, wide], operands, own_columns, after)
        return call(
            functools.partial(backward_middle, tick),
            "backward_middle",
            [shape_of(2 * ROWS + 8, WIDTH, dtype=F32), shape_of(4 * RING, DOT_ROWS, ROWS, dtype=F32)],
            operands=(mine, over(others, core_pairs()), saved, norm_gain, g, squares),
        )

    def backward_finish(tick, packed, dots, left, outs, *after):
        operands = (packed, saved, dots, *left)
        return call(
            functools.partial(backward_end, tick), "backward_end", [low, row, *outs], operands=operands, after=after
        )

    g, back_pieces = backward_begin(0, [returning[0]])
    gated = gate(back_pieces)
    back_landed = swapped(gated, rings())

    x, squares, pieces = forward_begin(0, [arriving[0]], gated)
    gated = gate(pieces, back_landed)
    landed = swapped(gated, rings())

    half = (value_local, (WIDTH, HALF), lambda i, scalars: (0, 1 - scalars[CORE_AT]))
    back_copies, half = turn("backward", back_landed, half, gated)
    value_other = over(half, core_pairs())
    gated = gate(back_copies, landed)
    back_gathered = swapped(gated, rings())

    half = (output_local, (HALF, WIDTH), lambda i, scalars: (1 - scalars[CORE_AT], 0))
    copies, half = turn("forward", landed, half, gated)
    output_other = over(half, core_pairs())
    packed, dots = backward_dots(0, back_gathered, g, squares, copies)
    all_dots = swapped(dots)

    gated = gate(copies, all_dots)
    gathered = swapped(gated, rings())

    input_grad, gain_total, totals = backward_finish(0, packed, all_dots, (), [small], gated)
    g, back_pieces = backward_begin(1, [shifted(input_grad, "segment", -1), cotangents])
    gated = gate(back_pieces, gathered)
    back_landed = swapped(gated, rings())

    operands = (x, *forward_product_of(gathered, gated), totals)
    (segment_out,) = call(forward_end, "forward_end", [low], operands=operands)
    x, squares, pieces = forward_begin(1, [shifted(segment_out, "segment", 1), fresh_inputs])
    gated = gate(pieces, back_landed)
    landed = swapped(gated, rings())

    (back_copies,) = turn("backward", back_landed, None, gated)
    gated = gate(back_copies, landed)
    back_gathered = swapped(gated, rings())

    (copies,) = turn("forward", landed, None, gated)
    gated = gate(copies, back_gathered)
    gathered = swapped(gated, rings())

    packed, dots = backward_dots(1, back_gathered, g, squares, gated)
    gated = gate(dots, gathered)
    all_dots = swapped(gated)

    left = (totals, gain_total, x, *forward_product_of(gathered, gated))
    input_grad, gain_total, segment_out = backward_finish(1, packed, all_dots, left, [low])
    return (segment_out[None], input_grad[None], gain_total)


def solution(mesh):
    return jax.shard_map(
        shards,
        mesh=mesh,
        in_specs=(
            P("segment", "shard", None),
            P("segment", None, "shard"),
            P("segment", "shard"),
            P("segment", None, "shard"),
            P(None, None, "shard"),
            P("segment", None, "shard"),
            P(None, None, "shard"),
            P("segment", None, None, "shard"),
            P("segment", None, None, "shard"),
            P("segment", None, None, "shard"),
            P(),
            P("segment", None, "shard"),
            P("segment", None, "shard"),
        ),
        out_specs=(P("segment", None, "shard"), P("segment", None, "shard"), P("segment", "shard")),
        check_vma=False,
    )
```

```python
import functools

import jax
import jax.numpy as jnp
from jax import lax
from jax.experimental import pallas as pl
from jax.experimental.pallas import tpu as pltpu
from jax.sharding import PartitionSpec as P

D = 8192
BLOCK = 128
ROWS = 128
WIDTH = 256
SEQ = 64
RING = 8
HALF = RING * WIDTH
EPSILON = 1e-05
F32 = jnp.float32
BF16 = jnp.bfloat16
VMEM_LIMIT = 20 * 1024 * 1024
DOT_ROWS = 8
SEGMENT_AT, CORE_AT, FORWARD_AT, BACKWARD_AT = 34, 35, 36, 40


def core_pairs():
    return [(index, index ^ 1) for index in range(4 * RING)]


def z_pairs():
    return [(index, index ^ 2) for index in range(4 * RING)]


def rings():
    return [[4 * y + rest for y in range(RING)] for rest in range(4)]


def swapped(value, groups=None):
    return lax.all_to_all(value, "shard", 0, 0, axis_index_groups=groups, tiled=True)


def gate(value, *after):
    return lax.optimization_barrier((value, *after))[0]


def shifted(value, axis, steps):
    count = lax.axis_size(axis)
    leading, last = (max(0, -steps), min(count, count - steps))
    return lax.ppermute(value, axis, [(source, source + steps) for source in range(leading, last)])


def call(kernel, name, outs, *, prefetch=(), blocks=None, operands=(), after=()):
    blocks = blocks or {}
    first, last = len(prefetch) + len(operands), len(prefetch) + len(operands) + len(after)

    def body(*refs):
        kernel(*refs[:first], *refs[last:])

    def spec(position, operand):
        if position in blocks:
            shape, index_map = blocks[position]
            return pl.BlockSpec(shape, index_map)
        rank = len(operand.shape)
        return pl.BlockSpec(operand.shape, lambda *_: (0,) * rank)

    in_specs = [spec(position, operand) for position, operand in enumerate(operands)]
    return pl.pallas_call(
        body,
        out_shape=outs,
        grid_spec=pltpu.PrefetchScalarGridSpec(
            num_scalar_prefetch=len(prefetch),
            grid=(1,),
            in_specs=in_specs + [pl.BlockSpec(memory_space=pl.ANY)] * len(after),
            out_specs=[pl.BlockSpec(out.shape, lambda *_, rank=len(out.shape): (0,) * rank) for out in outs],
        ),
        compiler_params=pltpu.CompilerParams(vmem_limit_bytes=VMEM_LIMIT),
        cost_estimate=pl.CostEstimate(flops=0, bytes_accessed=0, transcendentals=0),
        name=name,
    )(*prefetch, *operands, *after)


def shape_of(*dims, dtype=BF16):
    return jax.ShapeDtypeStruct(dims, dtype)


def across(column):
    return jnp.broadcast_to(column, (ROWS, ROWS)).T[0:1]


def down(row):
    square = jnp.broadcast_to(row, (ROWS, ROWS)).T
    return jnp.concatenate([square, square], axis=1)


def power_row(low, high, sign):
    lane = lax.broadcasted_iota(jnp.int32, (1, WIDTH), 1)
    exponent = sign * jnp.where(lane < BLOCK, low, high)
    magnitude = jnp.abs(exponent)
    grown = jnp.ones((1, WIDTH), F32)
    shrunk = jnp.ones((1, WIDTH), F32)
    for bit in range(4):
        bit_set = (magnitude >> bit) & 1 == 1
        grown = jnp.where(bit_set, grown * 2.0 ** (2**bit), grown)
        shrunk = jnp.where(bit_set, shrunk * 0.5 ** (2**bit), shrunk)
    return jnp.where(exponent < 0, shrunk, grown)


def decoded(message, first_ref, second_ref, scalars, at):
    low, high = scalars[at], scalars[at + 1]
    scale = power_row(low, high, 1)
    inverse = power_row(low, high, -1)
    base = jnp.concatenate([first_ref[0], second_ref[0]], axis=0).astype(F32)
    delta = jnp.clip((message.astype(F32) - base) * inverse, -127.0, 127.0).astype(BF16)
    return (base + delta.astype(F32) * scale).astype(BF16)


def chosen(scalars, edge, refs):
    if len(refs) == 1:
        return refs[0][...]
    return jnp.where(scalars[SEGMENT_AT] == edge, refs[1][0].astype(F32), refs[0][...].astype(F32))


def forward_start(tick, messages, scalars, *refs):
    given, (first, second, gain, weight, x_out, keep, send, squares) = refs[:messages], refs[messages:]
    x = decoded(chosen(scalars, 0, given), first, second, scalars, FORWARD_AT + 2 * tick)
    x_out[...] = x
    x = x.astype(F32)
    scaled = (x * gain[...]).astype(BF16)
    squares[...] = jnp.broadcast_to(across(jnp.sum(x * x, axis=1, keepdims=True)), squares.shape)
    core = scalars[CORE_AT]
    for out, half in ((send, 1 - core), (keep, core)):
        for j in range(RING):
            at = pl.multiple_of((half * RING + j) * WIDTH, WIDTH)
            part = jnp.dot(scaled, weight[:, pl.ds(at, WIDTH)], preferred_element_type=F32)
            out[j] = part.astype(BF16)


def backward_start(tick, messages, last, scalars, *refs):
    given, (first, second, weight, g_out, keep, send) = refs[:messages], refs[messages:]
    g = decoded(chosen(scalars, last, given), first, second, scalars, BACKWARD_AT + 2 * tick)
    g_out[...] = g
    core = scalars[CORE_AT]
    for out, half in ((send, 1 - core), (keep, core)):
        for j in range(RING):
            at = pl.multiple_of((half * RING + j) * WIDTH, WIDTH)
            part = lax.dot_general(
                g, weight[pl.ds(at, WIDTH), :], (((1,), (1,)), ((), ())), preferred_element_type=F32
            )
            out[j] = part.astype(BF16)


def core_sum(mine, other, out):
    for j in range(RING):
        out[j] = (mine[j].astype(F32) + other[j].astype(F32)).astype(BF16)


def ring_sum(pieces, out):
    total = pieces[0].astype(F32)
    for j in range(1, RING):
        total = total + pieces[j].astype(F32)
    out[...] = total.astype(BF16)


def share(own, other, *refs):
    value = (own[...].astype(F32) + other[...].astype(F32)).astype(BF16)
    out, *half = refs[len(refs) // 2 :]
    out[...] = jnp.broadcast_to(value[None], out.shape)
    if half:
        half[0][...] = refs[0][...]


def forward_product(blocks, own_weight, other_weight, mine, others):
    for weight, out in ((other_weight, others), (own_weight, mine)):
        total = jnp.zeros((ROWS, WIDTH), F32)
        for j in range(RING):
            rows = weight[j * WIDTH : (j + 1) * WIDTH, :]
            total = total + jnp.dot(blocks[j], rows, preferred_element_type=F32)
        out[...] = total


def backward_product(blocks, own_weight, other_weight, mine, others):
    for weight, out in ((other_weight, others), (own_weight, mine)):
        total = jnp.zeros((ROWS, WIDTH), F32)
        for j in range(RING):
            columns = weight[:, j * WIDTH : (j + 1) * WIDTH]
            total = total + lax.dot_general(
                blocks[j], columns, (((1,), (1,)), ((), ())), preferred_element_type=F32
            )
        out[...] = total


def row_factor(squares):
    return down(lax.rsqrt(squares / D + EPSILON))


def forward_sum(x, mine, other, squares):
    return (x[...].astype(F32) + row_factor(squares) * (mine[...] + other[...])).astype(BF16)


def forward_end(x, mine, other, totals, out):
    out[...] = forward_sum(x, mine, other, totals[3:4])


def backward_middle(tick, mine, other, saved, gain, g, squares, packed, dots):
    value = mine[...] + other[...]
    packed[:ROWS] = value
    packed[ROWS : 2 * ROWS] = g[...].astype(F32)
    packed[2 * ROWS :] = jnp.broadcast_to(gain[...], (8, WIDTH))
    terms = [saved[tick].astype(F32) * gain[...] * value]
    if tick == 0:
        for k in range(2):
            kept = saved[k].astype(F32)
            terms.append(kept * kept)
    rows = [across(jnp.sum(term, axis=1, keepdims=True)) for term in terms]
    rows += [jnp.zeros((1, ROWS), F32)] * (3 - len(rows))
    rows += [squares[:1], jnp.zeros((DOT_ROWS - 4, ROWS), F32)]
    dots[...] = jnp.broadcast_to(jnp.concatenate(rows, axis=0)[None], dots.shape)


def backward_end(tick, packed, saved, dots, *refs):
    total = dots[0]
    for j in range(1, dots.shape[0]):
        total = total + dots[j]
    if tick == 0:
        out, gain_out, totals = refs
        totals[...] = total
        squares = total[1:2]
    else:
        before, gain_before, x, mine, other, out, gain_out, segment_out = refs
        segment_out[...] = forward_sum(x, mine, other, total[3:4])
        squares = before[2:3]
    factor = row_factor(squares)
    kept = saved[tick].astype(F32)
    scaled_grad, g, gain = packed[:ROWS], packed[ROWS : 2 * ROWS], packed[2 * ROWS : 2 * ROWS + 1]
    sums = jnp.sum(scaled_grad * kept * factor, axis=0, keepdims=True)
    gain_out[...] = sums + gain_before[...] if tick else sums
    value = g + factor * gain * scaled_grad
    out[...] = (value - kept * (factor * factor * factor) * down(total[0:1]) / D).astype(BF16)


def flat(values):
    rows, columns = values.shape
    position = jnp.arange(rows)[:, None] * columns + jnp.arange(columns)[None, :]
    chosen_one = jnp.arange(rows * columns)[:, None, None] == position[None]
    return jnp.sum(jnp.where(chosen_one, values[None], 0), axis=(1, 2)).astype(jnp.int32)


def over(value, pairs):
    return lax.ppermute(value, "shard", pairs)


def shards(
    value_weight,
    output_weight,
    norm_gain,
    arriving,
    fresh_inputs,
    returning,
    cotangents,
    saved_inputs,
    forward_base,
    backward_base,
    sample_ids,
    forward_exponents,
    backward_exponents,
):
    segment = lax.axis_index("segment")
    segments = lax.axis_size("segment")
    position = lax.axis_index("shard")
    core = position % 2
    place = jnp.stack([segment, core]).astype(jnp.int32)
    exponents = flat(forward_exponents[0]), flat(backward_exponents[0])
    scalars = jnp.concatenate([flat(sample_ids), place, *exponents])
    value_local, output_local = value_weight[0], output_weight[0]
    saved = saved_inputs[0]
    low = shape_of(ROWS, WIDTH)
    wide = shape_of(ROWS, WIDTH, dtype=F32)
    eight = shape_of(RING, ROWS, WIDTH)
    row = shape_of(1, WIDTH, dtype=F32)
    small = shape_of(DOT_ROWS, ROWS, dtype=F32)
    own_half = {1: ((HALF, WIDTH), lambda i, scalars: (scalars[CORE_AT], 0))}
    own_columns = {1: ((WIDTH, HALF), lambda i, scalars: (0, scalars[CORE_AT]))}

    def base_blocks(first, micro):
        return {
            first + sample: (
                (1, SEQ, WIDTH),
                lambda i, scalars, sample=sample: (scalars[2 * micro(scalars[SEGMENT_AT]) + sample], 0, 0),
            )
            for sample in range(2)
        }

    def run(kernel, name, outs, operands, blocks=None, after=()):
        return call(kernel, name, outs, prefetch=(scalars,), operands=operands, blocks=blocks, after=after)

    def plain(kernel):
        return lambda _, *refs: kernel(*refs)

    def forward_begin(tick, messages, *after):
        count = len(messages)
        x, keep, send, squares = run(
            functools.partial(forward_start, tick, count),
            "forward_start",
            [low, eight, eight, small],
            (*messages, forward_base[0], forward_base[0], norm_gain, value_local),
            base_blocks(count, lambda segment: tick - segment + segments - 1),
            after,
        )
        operands = (keep, over(send, core_pairs()))
        return x, squares, *call(core_sum, "forward_core_sum", [eight], operands=operands)

    def backward_begin(tick, messages, *after):
        count = len(messages)
        g, keep, send = run(
            functools.partial(backward_start, tick, count, segments - 1),
            "backward_start",
            [low, eight, eight],
            (*messages, backward_base[0], backward_base[0], output_local),
            base_blocks(count, lambda segment: tick + segment),
            after,
        )
        operands = (keep, over(send, core_pairs()))
        return g, *call(core_sum, "backward_core_sum", [eight], operands=operands)

    def turn(name, pieces, half, *after):
        (own,) = call(ring_sum, name + "_ring_sum", [low], operands=(pieces,), after=after)
        operands, outs, blocks = (own, over(own, z_pairs())), [eight], {}
        if half:
            weight, shape, index_map = half
            operands, outs, blocks = (*operands, weight), [eight, shape_of(*shape)], {2: (shape, index_map)}
        return run(plain(share), name + "_share", outs, operands, blocks)

    def forward_product_of(gathered, *after):
        operands = (gathered, output_local, output_other)
        mine, others = run(plain(forward_product), "forward_product", [wide, wide], operands, own_half, after)
        return mine, over(others, core_pairs())

    def backward_dots(tick, gathered, g, squares, *after):
        operands = (gathered, value_local, value_other)
        mine, others = run(plain(backward_product), "backward_product", [wide, wide], operands, own_columns, after)
        return call(
            functools.partial(backward_middle, tick),
            "backward_middle",
            [shape_of(2 * ROWS + 8, WIDTH, dtype=F32), shape_of(4 * RING, DOT_ROWS, ROWS, dtype=F32)],
            operands=(mine, over(others, core_pairs()), saved, norm_gain, g, squares),
        )

    def backward_finish(tick, packed, dots, left, outs, *after):
        operands = (packed, saved, dots, *left)
        return call(
            functools.partial(backward_end, tick), "backward_end", [low, row, *outs], operands=operands, after=after
        )

    g, back_pieces = backward_begin(0, [returning[0]])
    gated = gate(back_pieces)
    back_landed = swapped(gated, rings())

    x, squares, pieces = forward_begin(0, [arriving[0]], gated)
    gated = gate(pieces, back_landed)
    landed = swapped(gated, rings())

    half = (value_local, (WIDTH, HALF), lambda i, scalars: (0, 1 - scalars[CORE_AT]))
    back_copies, half = turn("backward", back_landed, half, gated)
    value_other = over(half, core_pairs())
    gated = gate(back_copies, landed)
    back_gathered = swapped(gated, rings())

    half = (output_local, (HALF, WIDTH), lambda i, scalars: (1 - scalars[CORE_AT], 0))
    copies, half = turn("forward", landed, half, gated)
    output_other = over(half, core_pairs())
    packed, dots = backward_dots(0, back_gathered, g, squares, copies)
    all_dots = swapped(dots)

    gated = gate(copies, all_dots)
    gathered = swapped(gated, rings())

    input_grad, gain_total, totals = backward_finish(0, packed, all_dots, (), [small], gated)
    g, back_pieces = backward_begin(1, [shifted(input_grad, "segment", -1), cotangents])
    gated = gate(back_pieces, gathered)
    back_landed = swapped(gated, rings())

    operands = (x, *forward_product_of(gathered, gated), totals)
    (segment_out,) = call(forward_end, "forward_end", [low], operands=operands)
    x, squares, pieces = forward_begin(1, [shifted(segment_out, "segment", 1), fresh_inputs])
    gated = gate(pieces, back_landed)
    landed = swapped(gated, rings())

    (back_copies,) = turn("backward", back_landed, None, gated)
    gated = gate(back_copies, landed)
    back_gathered = swapped(gated, rings())

    (copies,) = turn("forward", landed, None, gated)
    gated = gate(copies, back_gathered)
    gathered = swapped(gated, rings())

    packed, dots = backward_dots(1, back_gathered, g, squares, gated)
    gated = gate(dots, gathered)
    all_dots = swapped(gated)

    left = (totals, gain_total, x, *forward_product_of(gathered, gated))
    input_grad, gain_total, segment_out = backward_finish(1, packed, all_dots, left, [low])
    return (segment_out[None], input_grad[None], gain_total)


def solution(mesh):
    return jax.shard_map(
        shards,
        mesh=mesh,
        in_specs=(
            P("segment", "shard", None),
            P("segment", None, "shard"),
            P("segment", "shard"),
            P("segment", None, "shard"),
            P(None, None, "shard"),
            P("segment", None, "shard"),
            P(None, None, "shard"),
            P("segment", None, None, "shard"),
            P("segment", None, None, "shard"),
            P("segment", None, None, "shard"),
            P(),
            P("segment", None, "shard"),
            P("segment", None, "shard"),
        ),
        out_specs=(P("segment", None, "shard"), P("segment", None, "shard"), P("segment", "shard")),
        check_vma=False,
    )
```

```python
import functools

import jax
import jax.numpy as jnp
from jax import lax
from jax.experimental import pallas as pl
from jax.experimental.pallas import tpu as pltpu
from jax.sharding import PartitionSpec as P

D = 8192
BLOCK = 128
ROWS = 128
WIDTH = 256
SEQ = 64
RING = 8
HALF = RING * WIDTH
EPSILON = 1e-05
F32 = jnp.float32
BF16 = jnp.bfloat16
VMEM_LIMIT = 20 * 1024 * 1024
DOT_ROWS = 8
SEGMENT_AT, CORE_AT, FORWARD_AT, BACKWARD_AT = 34, 35, 36, 40


def core_pairs():
    return [(index, index ^ 1) for index in range(4 * RING)]


def z_pairs():
    return [(index, index ^ 2) for index in range(4 * RING)]


def rings():
    return [[4 * y + rest for y in range(RING)] for rest in range(4)]


def swapped(value, groups=None):
    return lax.all_to_all(value, "shard", 0, 0, axis_index_groups=groups, tiled=True)


def gate(value, *after):
    return lax.optimization_barrier((value, *after))[0]


def shifted(value, axis, steps):
    count = lax.axis_size(axis)
    leading, last = (max(0, -steps), min(count, count - steps))
    return lax.ppermute(value, axis, [(source, source + steps) for source in range(leading, last)])


def call(kernel, name, outs, *, prefetch=(), blocks=None, operands=(), after=()):
    blocks = blocks or {}
    first, last = len(prefetch) + len(operands), len(prefetch) + len(operands) + len(after)

    def body(*refs):
        kernel(*refs[:first], *refs[last:])

    def spec(position, operand):
        if position in blocks:
            shape, index_map = blocks[position]
            return pl.BlockSpec(shape, index_map)
        rank = len(operand.shape)
        return pl.BlockSpec(operand.shape, lambda *_: (0,) * rank)

    in_specs = [spec(position, operand) for position, operand in enumerate(operands)]
    return pl.pallas_call(
        body,
        out_shape=outs,
        grid_spec=pltpu.PrefetchScalarGridSpec(
            num_scalar_prefetch=len(prefetch),
            grid=(1,),
            in_specs=in_specs + [pl.BlockSpec(memory_space=pl.ANY)] * len(after),
            out_specs=[pl.BlockSpec(out.shape, lambda *_, rank=len(out.shape): (0,) * rank) for out in outs],
        ),
        compiler_params=pltpu.CompilerParams(vmem_limit_bytes=VMEM_LIMIT),
        cost_estimate=pl.CostEstimate(flops=0, bytes_accessed=0, transcendentals=0),
        name=name,
    )(*prefetch, *operands, *after)


def shape_of(*dims, dtype=BF16):
    return jax.ShapeDtypeStruct(dims, dtype)


def across(column):
    return jnp.broadcast_to(column, (ROWS, ROWS)).T[0:1]


def down(row):
    square = jnp.broadcast_to(row, (ROWS, ROWS)).T
    return jnp.concatenate([square, square], axis=1)


def power_row(low, high, sign):
    lane = lax.broadcasted_iota(jnp.int32, (1, WIDTH), 1)
    exponent = sign * jnp.where(lane < BLOCK, low, high)
    magnitude = jnp.abs(exponent)
    grown = jnp.ones((1, WIDTH), F32)
    shrunk = jnp.ones((1, WIDTH), F32)
    for bit in range(4):
        bit_set = (magnitude >> bit) & 1 == 1
        grown = jnp.where(bit_set, grown * 2.0 ** (2**bit), grown)
        shrunk = jnp.where(bit_set, shrunk * 0.5 ** (2**bit), shrunk)
    return jnp.where(exponent < 0, shrunk, grown)


def decoded(message, first_ref, second_ref, scalars, at):
    low, high = scalars[at], scalars[at + 1]
    scale = power_row(low, high, 1)
    inverse = power_row(low, high, -1)
    base = jnp.concatenate([first_ref[0], second_ref[0]], axis=0).astype(F32)
    delta = jnp.clip((message.astype(F32) - base) * inverse, -127.0, 127.0).astype(BF16)
    return (base + delta.astype(F32) * scale).astype(BF16)


def chosen(scalars, edge, refs):
    if len(refs) == 1:
        return refs[0][...]
    return jnp.where(scalars[SEGMENT_AT] == edge, refs[1][0].astype(F32), refs[0][...].astype(F32))


def forward_start(tick, messages, scalars, *refs):
    given, (first, second, gain, weight, x_out, keep, send, squares) = refs[:messages], refs[messages:]
    x = decoded(chosen(scalars, 0, given), first, second, scalars, FORWARD_AT + 2 * tick)
    x_out[...] = x
    x = x.astype(F32)
    scaled = (x * gain[...]).astype(BF16)
    squares[...] = jnp.broadcast_to(across(jnp.sum(x * x, axis=1, keepdims=True)), squares.shape)
    core = scalars[CORE_AT]
    for out, half in ((send, 1 - core), (keep, core)):
        for j in range(RING):
            at = pl.multiple_of((half * RING + j) * WIDTH, WIDTH)
            part = jnp.dot(scaled, weight[:, pl.ds(at, WIDTH)], preferred_element_type=F32)
            out[j] = part.astype(BF16)


def backward_start(tick, messages, last, scalars, *refs):
    given, (first, second, weight, g_out, keep, send) = refs[:messages], refs[messages:]
    g = decoded(chosen(scalars, last, given), first, second, scalars, BACKWARD_AT + 2 * tick)
    g_out[...] = g
    core = scalars[CORE_AT]
    for out, half in ((send, 1 - core), (keep, core)):
        for j in range(RING):
            at = pl.multiple_of((half * RING + j) * WIDTH, WIDTH)
            part = lax.dot_general(
                g, weight[pl.ds(at, WIDTH), :], (((1,), (1,)), ((), ())), preferred_element_type=F32
            )
            out[j] = part.astype(BF16)


def core_sum(mine, other, out):
    for j in range(RING):
        out[j] = (mine[j].astype(F32) + other[j].astype(F32)).astype(BF16)


def ring_sum(pieces, out):
    total = pieces[0].astype(F32)
    for j in range(1, RING):
        total = total + pieces[j].astype(F32)
    out[...] = total.astype(BF16)


def share(own, other, *refs):
    value = (own[...].astype(F32) + other[...].astype(F32)).astype(BF16)
    out, *half = refs[len(refs) // 2 :]
    out[...] = jnp.broadcast_to(value[None], out.shape)
    if half:
        half[0][...] = refs[0][...]


def copied(weight, out):
    out[...] = weight[...]


def forward_product(blocks, own_weight, other_weight, mine, others):
    for weight, out in ((other_weight, others), (own_weight, mine)):
        total = jnp.zeros((ROWS, WIDTH), F32)
        for j in range(RING):
            rows = weight[j * WIDTH : (j + 1) * WIDTH, :]
            total = total + jnp.dot(blocks[j], rows, preferred_element_type=F32)
        out[...] = total


def backward_product(blocks, own_weight, other_weight, mine, others):
    for weight, out in ((other_weight, others), (own_weight, mine)):
        total = jnp.zeros((ROWS, WIDTH), F32)
        for j in range(RING):
            columns = weight[:, j * WIDTH : (j + 1) * WIDTH]
            total = total + lax.dot_general(
                blocks[j], columns, (((1,), (1,)), ((), ())), preferred_element_type=F32
            )
        out[...] = total


def row_factor(squares):
    return down(lax.rsqrt(squares / D + EPSILON))


def forward_sum(x, mine, other, squares):
    return (x[...].astype(F32) + row_factor(squares) * (mine[...] + other[...])).astype(BF16)


def forward_end(x, mine, other, totals, out):
    out[...] = forward_sum(x, mine, other, totals[3:4])


def backward_middle(tick, mine, other, saved, gain, g, squares, packed, dots):
    value = mine[...] + other[...]
    packed[:ROWS] = value
    packed[ROWS : 2 * ROWS] = g[...].astype(F32)
    packed[2 * ROWS :] = jnp.broadcast_to(gain[...], (8, WIDTH))
    terms = [saved[tick].astype(F32) * gain[...] * value]
    if tick == 0:
        for k in range(2):
            kept = saved[k].astype(F32)
            terms.append(kept * kept)
    rows = [across(jnp.sum(term, axis=1, keepdims=True)) for term in terms]
    rows += [jnp.zeros((1, ROWS), F32)] * (3 - len(rows))
    rows += [squares[:1], jnp.zeros((DOT_ROWS - 4, ROWS), F32)]
    dots[...] = jnp.broadcast_to(jnp.concatenate(rows, axis=0)[None], dots.shape)


def backward_end(tick, packed, saved, dots, *refs):
    total = dots[0]
    for j in range(1, dots.shape[0]):
        total = total + dots[j]
    if tick == 0:
        out, gain_out, totals = refs
        totals[...] = total
        squares = total[1:2]
    else:
        before, gain_before, x, mine, other, out, gain_out, segment_out = refs
        segment_out[...] = forward_sum(x, mine, other, total[3:4])
        squares = before[2:3]
    factor = row_factor(squares)
    kept = saved[tick].astype(F32)
    scaled_grad, g, gain = packed[:ROWS], packed[ROWS : 2 * ROWS], packed[2 * ROWS : 2 * ROWS + 1]
    sums = jnp.sum(scaled_grad * kept * factor, axis=0, keepdims=True)
    gain_out[...] = sums + gain_before[...] if tick else sums
    value = g + factor * gain * scaled_grad
    out[...] = (value - kept * (factor * factor * factor) * down(total[0:1]) / D).astype(BF16)


def flat(values):
    rows, columns = values.shape
    position = jnp.arange(rows)[:, None] * columns + jnp.arange(columns)[None, :]
    chosen_one = jnp.arange(rows * columns)[:, None, None] == position[None]
    return jnp.sum(jnp.where(chosen_one, values[None], 0), axis=(1, 2)).astype(jnp.int32)


def over(value, pairs):
    return lax.ppermute(value, "shard", pairs)


def shards(
    value_weight,
    output_weight,
    norm_gain,
    arriving,
    fresh_inputs,
    returning,
    cotangents,
    saved_inputs,
    forward_base,
    backward_base,
    sample_ids,
    forward_exponents,
    backward_exponents,
):
    segment = lax.axis_index("segment")
    segments = lax.axis_size("segment")
    position = lax.axis_index("shard")
    core = position % 2
    place = jnp.stack([segment, core]).astype(jnp.int32)
    exponents = flat(forward_exponents[0]), flat(backward_exponents[0])
    scalars = jnp.concatenate([flat(sample_ids), place, *exponents])
    value_local, output_local = value_weight[0], output_weight[0]
    saved = saved_inputs[0]
    low = shape_of(ROWS, WIDTH)
    wide = shape_of(ROWS, WIDTH, dtype=F32)
    eight = shape_of(RING, ROWS, WIDTH)
    row = shape_of(1, WIDTH, dtype=F32)
    small = shape_of(DOT_ROWS, ROWS, dtype=F32)
    own_half = {1: ((HALF, WIDTH), lambda i, scalars: (scalars[CORE_AT], 0))}
    own_columns = {1: ((WIDTH, HALF), lambda i, scalars: (0, scalars[CORE_AT]))}

    def base_blocks(first, micro):
        return {
            first + sample: (
                (1, SEQ, WIDTH),
                lambda i, scalars, sample=sample: (scalars[2 * micro(scalars[SEGMENT_AT]) + sample], 0, 0),
            )
            for sample in range(2)
        }

    def run(kernel, name, outs, operands, blocks=None, after=()):
        return call(kernel, name, outs, prefetch=(scalars,), operands=operands, blocks=blocks, after=after)

    def plain(kernel):
        return lambda _, *refs: kernel(*refs)

    def forward_begin(tick, messages, *after):
        count = len(messages)
        x, keep, send, squares = run(
            functools.partial(forward_start, tick, count),
            "forward_start",
            [low, eight, eight, small],
            (*messages, forward_base[0], forward_base[0], norm_gain, value_local),
            base_blocks(count, lambda segment: tick - segment + segments - 1),
            after,
        )
        operands = (keep, over(send, core_pairs()))
        return x, squares, *call(core_sum, "forward_core_sum", [eight], operands=operands)

    def backward_begin(tick, messages, *after):
        count = len(messages)
        g, keep, send = run(
            functools.partial(backward_start, tick, count, segments - 1),
            "backward_start",
            [low, eight, eight],
            (*messages, backward_base[0], backward_base[0], output_local),
            base_blocks(count, lambda segment: tick + segment),
            after,
        )
        operands = (keep, over(send, core_pairs()))
        return g, *call(core_sum, "backward_core_sum", [eight], operands=operands)

    def turn(name, pieces, half, *after):
        (own,) = call(ring_sum, name + "_ring_sum", [low], operands=(pieces,), after=after)
        operands, outs, blocks = (own, over(own, z_pairs())), [eight], {}
        if half:
            weight, shape, index_map = half
            operands, outs, blocks = (*operands, weight), [eight, shape_of(*shape)], {2: (shape, index_map)}
        return run(plain(share), name + "_share", outs, operands, blocks)

    def forward_product_of(gathered, *after):
        operands = (gathered, output_local, output_other)
        mine, others = run(plain(forward_product), "forward_product", [wide, wide], operands, own_half, after)
        return mine, over(others, core_pairs())

    def backward_dots(tick, gathered, g, squares, *after):
        operands = (gathered, value_local, value_other)
        mine, others = run(plain(backward_product), "backward_product", [wide, wide], operands, own_columns, after)
        return call(
            functools.partial(backward_middle, tick),
            "backward_middle",
            [shape_of(2 * ROWS + 8, WIDTH, dtype=F32), shape_of(4 * RING, DOT_ROWS, ROWS, dtype=F32)],
            operands=(mine, over(others, core_pairs()), saved, norm_gain, g, squares),
        )

    def backward_finish(tick, packed, dots, left, outs, *after):
        operands = (packed, saved, dots, *left)
        return call(
            functools.partial(backward_end, tick), "backward_end", [low, row, *outs], operands=operands, after=after
        )

    g, back_pieces = backward_begin(0, [returning[0]])
    gated = gate(back_pieces)
    back_landed = swapped(gated, rings())

    x, squares, pieces = forward_begin(0, [arriving[0]], gated)
    own_rows = {0: ((HALF, WIDTH), lambda i, scalars: (1 - scalars[CORE_AT], 0))}
    (half,) = run(plain(copied), "half", [shape_of(HALF, WIDTH)], (output_local,), own_rows, (pieces,))
    output_other = over(half, core_pairs())
    gated = gate(pieces, back_landed, half)
    landed = swapped(gated, rings())

    half = (value_local, (WIDTH, HALF), lambda i, scalars: (0, 1 - scalars[CORE_AT]))
    back_copies, half = turn("backward", back_landed, half, gated)
    value_other = over(half, core_pairs())
    gated = gate(back_copies, landed)
    back_gathered = swapped(gated, rings())

    (copies,) = turn("forward", landed, None, gated)
    packed, dots = backward_dots(0, back_gathered, g, squares, copies)
    all_dots = swapped(dots)

    gated = gate(copies, all_dots)
    gathered = swapped(gated, rings())

    input_grad, gain_total, totals = backward_finish(0, packed, all_dots, (), [small], gated)
    g, back_pieces = backward_begin(1, [shifted(input_grad, "segment", -1), cotangents])
    gated = gate(back_pieces, gathered)
    back_landed = swapped(gated, rings())

    operands = (x, *forward_product_of(gathered, gated), totals)
    (segment_out,) = call(forward_end, "forward_end", [low], operands=operands)
    x, squares, pieces = forward_begin(1, [shifted(segment_out, "segment", 1), fresh_inputs])
    gated = gate(pieces, back_landed)
    landed = swapped(gated, rings())

    (back_copies,) = turn("backward", back_landed, None, gated)
    gated = gate(back_copies, landed)
    back_gathered = swapped(gated, rings())

    (copies,) = turn("forward", landed, None, gated)
    gated = gate(copies, back_gathered)
    gathered = swapped(gated, rings())

    packed, dots = backward_dots(1, back_gathered, g, squares, gated)
    gated = gate(dots, gathered)
    all_dots = swapped(gated)

    left = (totals, gain_total, x, *forward_product_of(gathered, gated))
    input_grad, gain_total, segment_out = backward_finish(1, packed, all_dots, left, [low])
    return (segment_out[None], input_grad[None], gain_total)


def solution(mesh):
    return jax.shard_map(
        shards,
        mesh=mesh,
        in_specs=(
            P("segment", "shard", None),
            P("segment", None, "shard"),
            P("segment", "shard"),
            P("segment", None, "shard"),
            P(None, None, "shard"),
            P("segment", None, "shard"),
            P(None, None, "shard"),
            P("segment", None, None, "shard"),
            P("segment", None, None, "shard"),
            P("segment", None, None, "shard"),
            P(),
            P("segment", None, "shard"),
            P("segment", None, "shard"),
        ),
        out_specs=(P("segment", None, "shard"), P("segment", None, "shard"), P("segment", "shard")),
        check_vma=False,
    )
```
